512 devices in a mesh: horiz: 64 (over x, z, core), lev: 8 (over y).
Axes of the slice: x: 4, y: 8, z: 8, core: 2. Of those that a mesh axis runs over, the one named last changes fastest.
Arguments:
- prior_state: float32 [80, 8, 262144], P(None, 'lev', 'horiz'), may hold values from -6 to 6
- localization: float32 [6, 128, 8, 2048], P(None, None, 'lev', 'horiz'), may hold values from 0.1 to 1
- observed: float32 [6, 128], replicated, may hold values from -5 to 5
- error_variance: float32 [6, 128], replicated, may hold values from 0.3 to 2
- owner_ids: int32 [6], replicated, may hold values from 0 to 63
- obs_cell: int32 [6, 128], replicated, may hold values from 0 to 4095
Outputs:
- posterior_state: float32 [80, 8, 262144], P(None, 'lev', 'horiz')
- obs_increments: float32 [6, 128, 80], replicated
The draws below stay inside these ranges and needn't reach their ends.
All inputs are finite; a program needn't handle non-finite values.
Results may differ from the reference program's by a relative error of at most 0.0001.
Values sent between devices are 32-bit elements; how exact they have to be, the bound alone decides.
A program may use at most 64 MiB of HBM per device.

```python
import math
import jax
import jax.numpy as jnp
from jax import lax

MEMBERS = 80
OBS = 128
BATCHES = 6
HC_DEV = 4096
TILE = 128
LEVELS = 8
HCELLS = 262144
HTILES = 2048
N_HORIZ = 64


def place_ends(entries, stream_key, least, high):
    index_at = [jax.random.randint(jax.random.fold_in(stream_key, axis), (), 0, length) for axis, length in enumerate(entries.shape)]
    main_axis = entries.shape.index(max(entries.shape))
    beside = index_at[:main_axis] + [(index_at[main_axis] + 1) % entries.shape[main_axis]] + index_at[main_axis + 1:]
    return entries.at[tuple(index_at)].set(least).at[tuple(beside)].set(high)


def block_levels(rng, dims, cuts, smallest, high):
    factor_of, own = 1.0, jax.random.fold_in(rng, 6)
    for dim, parts in cuts:
        heights = jnp.exp(jax.random.uniform(jax.random.fold_in(own, dim), (parts,), jnp.float32, smallest / len(cuts), high / len(cuts)))
        factor_of = factor_of * jnp.repeat(heights, dims[dim] // parts).reshape([-1 if axis == dim else 1 for axis in range(len(dims))])
    return factor_of


def centred(key, extent, scale, reach, split=(), kind=jnp.bfloat16):
    drawn = scale * jax.random.normal(key, extent, jnp.float32)
    if split:
        drawn = drawn * block_levels(key, extent, split, -0.22, 0.18)
    return jnp.clip(drawn, -reach, reach).astype(kind)


def setup_inputs(seed: int = 0) -> dict:
    keys = jax.random.split(jax.random.key(seed), 7)
    prior_state = centred(keys[0], (MEMBERS, LEVELS, HCELLS), 1.0, 6.0, ((1, 8), (2, 64)), jnp.float32)
    localization = jnp.clip(0.1 + 0.9 * jax.random.uniform(keys[1], (BATCHES, OBS, LEVELS, HTILES), jnp.float32) ** block_levels(keys[1], (BATCHES, OBS, LEVELS, HTILES), ((2, 8), (3, 64)), -0.2, 0.2), 0.1, 1.0)
    observed = centred(keys[2], (BATCHES, OBS), 1.0, 5.0, (), jnp.float32)
    error_variance = jnp.clip(jnp.exp(jax.random.uniform(keys[3], (BATCHES, OBS), jnp.float32, math.log(0.3), math.log(2.0))), 0.3, 2.0)
    owner_ids = place_ends(jax.random.randint(keys[4], (BATCHES,), 0, N_HORIZ), jax.random.fold_in(keys[4], 1), 0, N_HORIZ - 1).astype(jnp.int32)
    obs_cell = place_ends(jax.random.randint(keys[5], (BATCHES, OBS), 0, HC_DEV), jax.random.fold_in(keys[5], 1), 0, HC_DEV - 1).astype(jnp.int32)
    return dict(prior_state=prior_state, localization=localization, observed=observed, error_variance=error_variance, owner_ids=owner_ids, obs_cell=obs_cell)


highest = lax.Precision.HIGHEST

def batch_increment(priors, observed_now, variance):
    members = priors.shape[1]
    average = lax.optimization_barrier(jnp.mean(priors, axis=1))
    deviation = priors - average[:, None]
    covariance = jnp.dot(deviation, deviation.T, precision=highest) / (members - 1)
    factor = jnp.linalg.cholesky(covariance + jnp.diag(variance))
    innovation = observed_now - average
    half_solved = jax.scipy.linalg.solve_triangular(factor, innovation, lower=True)
    gain_vector = jax.scipy.linalg.solve_triangular(factor, half_solved, lower=True, trans=1)
    mean_shift = jnp.dot(covariance, gain_vector, precision=highest)
    rooted = factor + jnp.diag(jnp.sqrt(variance))
    whitened = jax.scipy.linalg.solve_triangular(rooted, deviation, lower=True)
    unwhitened = jax.scipy.linalg.solve_triangular(factor, whitened, lower=True, trans=1)
    increment = mean_shift[:, None] - jnp.dot(covariance, unwhitened, precision=highest)
    half_gain = jax.scipy.linalg.solve_triangular(factor, increment, lower=True)
    gain_weights = jax.scipy.linalg.solve_triangular(factor, half_gain, lower=True, trans=1)
    return (increment, gain_weights)

def regress(window, deviation, gain_weights, tile_weights):
    members, levels, span_cells = window.shape
    observations = deviation.shape[0]
    flattened = window.reshape(members, levels * span_cells)
    covariance = jnp.dot(deviation, flattened, precision=highest)
    scaled = covariance.reshape(observations, levels, span_cells // TILE, TILE) * (tile_weights / (members - 1.0))[..., None]
    update = jnp.dot(gain_weights.T, scaled.reshape(observations, levels * span_cells), precision=highest)
    return window + update.reshape(members, levels, span_cells)

def reference(prior_state, localization, observed, error_variance, owner_ids, obs_cell):
    ensemble = prior_state
    level_of = jnp.arange(OBS, dtype=jnp.int32) // (OBS // LEVELS)
    collected = []
    for batch_index in range(BATCHES):
        cell_index = (owner_ids[batch_index] * HC_DEV + obs_cell[batch_index]).astype(jnp.int32)
        priors = ensemble[:, level_of, cell_index].T
        increment, gain_weights = batch_increment(priors, observed[batch_index], error_variance[batch_index])
        deviation = priors - lax.optimization_barrier(jnp.mean(priors, axis=1))[:, None]
        weights = localization[batch_index]

        def column_block(position, current):
            offset = (position * HC_DEV).astype(jnp.int32)
            window = lax.dynamic_slice_in_dim(current, offset, HC_DEV, 2)
            tile_weights = lax.dynamic_slice_in_dim(weights, (position * (HC_DEV // TILE)).astype(jnp.int32), HC_DEV // TILE, 2)
            updated = regress(window, deviation, gain_weights, tile_weights)
            return lax.dynamic_update_slice_in_dim(current, updated, offset, 2)
        ensemble = lax.fori_loop(0, N_HORIZ, column_block, ensemble)
        collected.append(increment)
    return (ensemble, jnp.stack(collected))
```

```python
import jax, jax.numpy as jnp
from jax import lax
from jax.experimental import pallas as pl
from jax.experimental.pallas import tpu as pltpu
from jax.sharding import PartitionSpec as P
f32 = jnp.float32
bf16 = jnp.bfloat16
HI = lax.Precision.HIGHEST
MESH = pl.DeviceIdType.MESH
X_DIM, Z_DIM, Y_DIM = 4, 8, 8
COLUMNS = X_DIM * Z_DIM * 2
TILE = 128
N, M = 128, 80
PER_LEVEL = 16

def matrices(batches):
    return [(b, None if s == 0 else s - 1) for b in range(batches) for s in range(b + 1)]

def root(q):
    return (q + q // 8) % 4, q % 8, (q // 2) % 2

def rank(x, z, core):
    return (x * Z_DIM + z) * 2 + core

def extract_kernel(obs_cell, state, weights, send):
    batches = obs_cell.shape[0]
    lev = lax.axis_index("lev")
    tiles = weights.shape[1]
    lane = lax.broadcasted_iota(jnp.int32, (M, N), 1)
    for b in range(batches):
        base = b * (b + 1) // 2

        def observation(j, gathered):
            cell = obs_cell[b, lev * PER_LEVEL + j]
            tile, at = cell // TILE, cell % TILE
            chunk = state[pl.ds(tile, M, stride=tiles), :]
            gathered = jnp.where(lane == j, pltpu.roll(chunk, lax.rem(j - at + N, N), 1), gathered)
            for a in range(b):
                send[base + 1 + a, pl.ds(j, 1), :] = weights[a, pl.ds(tile, 1), :]
            return gathered
        gathered = lax.fori_loop(0, PER_LEVEL, observation, jnp.zeros((M, N), f32))
        square = jnp.concatenate([gathered, jnp.zeros((N - M, N), f32)], axis=0)
        send[base] = square.T[:PER_LEVEL]

def extract(obs_cell, state, weights):
    batches = obs_cell.shape[0]
    count = batches * (batches + 1) // 2
    vm = pl.BlockSpec(memory_space=pltpu.VMEM)
    return pl.pallas_call(extract_kernel,
        out_shape=jax.ShapeDtypeStruct((count, PER_LEVEL, N), f32),
        in_specs=[pl.BlockSpec(memory_space=pltpu.SMEM), vm, vm], out_specs=vm,
        compiler_params=pltpu.CompilerParams(vmem_limit_bytes=48 << 20),
    )(obs_cell, state, weights)

def comm_kernel(owner_ids, send, mats, slots, mine, slot_sem, own_sem, push_sem, level_sem, level_push, mat_sem, mat_push):
    count = send.shape[0]
    batches = owner_ids.shape[0]
    h, lev = lax.axis_index("horiz"), lax.axis_index("lev")
    x, z, core = h // (2 * Z_DIM), (h // 2) % Z_DIM, h % 2
    barrier = pltpu.get_barrier_semaphore()
    for step in range(1, COLUMNS):
        pl.semaphore_signal(barrier, inc=1, device_id={"horiz": (h + step) % COLUMNS, "lev": lev}, device_id_type=MESH)
    for step in range(1, Y_DIM):
        pl.semaphore_signal(barrier, inc=1, device_id={"horiz": h, "lev": (lev + step) % Y_DIM}, device_id_type=MESH)
    pl.semaphore_wait(barrier, COLUMNS + Y_DIM - 2)

    which = matrices(batches)
    roots = [rank(*root(q)) for q in range(count)]

    def push(q):
        return pltpu.make_async_remote_copy(send.at[q], slots.at[h], push_sem.at[q], slot_sem,
            device_id={"horiz": roots[q], "lev": lev}, device_id_type=MESH)

    def column(q):
        return pl.ds(pl.multiple_of(lev * PER_LEVEL, PER_LEVEL), PER_LEVEL)

    def level(q, step):
        return pltpu.make_async_remote_copy(mine, mats.at[q, column(q), :], level_push.at[step - 1], level_sem,
            device_id={"horiz": h, "lev": (lev + step) % Y_DIM}, device_id_type=MESH)

    def forward(q, slot, to):
        return pltpu.make_async_remote_copy(mats.at[q], mats.at[q], mat_push.at[q, slot], mat_sem.at[q],
            device_id={"horiz": to, "lev": lev}, device_id_type=MESH)

    def z_peers(q):
        return [(step - 1, rank(x, (z + step) % Z_DIM, core)) for step in range(1, Z_DIM)]

    def x_peers(q):
        return [(6 + step, rank((x + step) % X_DIM, z, core)) for step in range(1, X_DIM)]

    def core_peer(q):
        return [(10, rank(x, z, 1 - core))]

    for q in range(count):
        @pl.when(h != roots[q])
        def _():
            push(q).start()

    for q in range(count):
        @pl.when(h == roots[q])
        def _():
            own = pltpu.make_async_copy(send.at[q], slots.at[h], own_sem)
            own.start()
            own.wait()
            pltpu.make_async_copy(slots.at[1:], slots.at[1:], slot_sem).wait()
            owned = slots[owner_ids[which[q][0]]]
            mine[...] = owned
            for step in range(1, Y_DIM):
                level(q, step).start()
            mats[q, column(q), :] = owned
            for step in range(1, Y_DIM):
                level(q, step).wait_send()
            rows = pl.ds(0, (Y_DIM - 1) * PER_LEVEL)
            pltpu.make_async_copy(mats.at[q, rows, :], mats.at[q, rows, :], level_sem).wait()

    def each(q, then):
        rx, rz, rcore = root(q)
        @pl.when(h == roots[q])
        def _():
            for slot, to in z_peers(q):
                then(forward(q, slot, to))
        @pl.when((x == rx) & (core == rcore))
        def _():
            for slot, to in x_peers(q):
                then(forward(q, slot, to))
        @pl.when(core == rcore)
        def _():
            for slot, to in core_peer(q):
                then(forward(q, slot, to))

    for q in range(count):
        @pl.when(h != roots[q])
        def _():
            pltpu.make_async_copy(mats.at[q], mats.at[q], mat_sem.at[q]).wait()
        each(q, lambda copy: copy.start())
    for q in range(count):
        each(q, lambda copy: copy.wait_send())
        @pl.when(h != roots[q])
        def _():
            push(q).wait_send()

def share(owner_ids, send):
    count = send.shape[0]
    vm = pl.BlockSpec(memory_space=pltpu.VMEM)
    dma = pltpu.SemaphoreType.DMA
    return pl.pallas_call(comm_kernel,
        out_shape=jax.ShapeDtypeStruct((count, N, N), f32),
        in_specs=[pl.BlockSpec(memory_space=pltpu.SMEM), vm], out_specs=vm,
        scratch_shapes=[pltpu.VMEM((COLUMNS, PER_LEVEL, N), f32), pltpu.VMEM((PER_LEVEL, N), f32),
            dma, dma, dma((count,)), dma, dma((Y_DIM - 1,)), dma((count,)), dma((count, 11))],
        compiler_params=pltpu.CompilerParams(vmem_limit_bytes=48 << 20, collective_id=0, has_side_effects=True),
    )(owner_ids, send)

def dot(a, b, ca=1, cb=0, precision=HI):
    return lax.dot_general(a, b, (((ca,), (cb,)), ((), ())), precision=precision, preferred_element_type=f32)

def split3(x):
    h = x.astype(bf16).astype(f32)
    r = x - h
    m = r.astype(bf16).astype(f32)
    return h, m, r - m

def panel_product(left, right):
    h, m, l = split3(left)
    lhs = jnp.concatenate([h, h, m, m, h, l], axis=0).T.astype(bf16)
    h, m, l = split3(right)
    rhs = jnp.concatenate([h, m, h, m, l, h], axis=0).astype(bf16)
    return lax.dot_general(lhs, rhs, (((1,), (0,)), ((), ())), preferred_element_type=f32)

def eliminate(work, solved, root_col):
    row16 = lax.broadcasted_iota(jnp.int32, (16, N), 0)
    row8 = lax.broadcasted_iota(jnp.int32, (8, N), 0)
    lane1 = lax.broadcasted_iota(jnp.int32, (1, N), 1)
    for block in range(N // 8):
        r0 = 8 * block
        tall = 16 if block < N // 8 - 1 else 8
        rows = row16[:tall]
        win_s = work[r0:r0 + tall, 0:N]
        win_a = work[r0:r0 + tall, N:2 * N]
        win_d = work[r0:r0 + tall, 2 * N:3 * N]
        roots = jnp.broadcast_to(root_col[r0:r0 + 8, :], (8, N))
        cols = [jnp.broadcast_to(win_s[:, r0 + k:r0 + k + 1], (tall, N)) for k in range(8)]
        diag = jnp.ones((8, N), f32)
        used_d = jnp.zeros((8, N), f32)
        for j in range(8):
            d = cols[j][j:j + 1, :]
            g = jnp.where(rows > j, cols[j] * (1.0 / d), 0.0)
            for k in range(j + 1, 8):
                cols[k] = cols[k] - g * cols[k][j:j + 1, :]
            win_s = win_s - g * win_s[j:j + 1, :]
            win_a = win_a - g * win_a[j:j + 1, :]
            f = jnp.sqrt(d)
            s = jnp.where(lane1 < M, f / (f + roots[j:j + 1, :]), 1.0)
            scaled = win_d[j:j + 1, :] * s
            win_d = win_d - g * scaled
            diag = jnp.where(row8 == j, d, diag)
            used_d = jnp.where(row8 == j, scaled, used_d)
        if block < N // 8 - 1:
            work[r0 + 8:r0 + 16, 0:N] = win_s[8:]
            work[r0 + 8:r0 + 16, N:2 * N] = win_a[8:]
            work[r0 + 8:r0 + 16, 2 * N:3 * N] = win_d[8:]
        inv = lax.rsqrt(diag)
        f = diag * inv
        solved[r0:r0 + 8, 0:N] = win_a[:8] * inv
        v = jnp.broadcast_to(win_d[:8, M:M + 1], (8, N)) * inv
        solved[r0:r0 + 8, N:2 * N] = jnp.where(lane1 < M, v - win_d[:8] / (f + roots), 0.0)
        if r0 + 16 < N:
            right = jnp.concatenate([win_s[:8], win_a[:8], used_d], axis=1)
            update = panel_product(win_s[:8] / diag, right)
            work[r0 + 16:, :] = work[r0 + 16:, :] - update[r0 + 16:, :]

def chain_kernel(mats, observed, variance, state, local_w, post_out, incs, work, solved, cur, post, state_sem):
    batches = observed.shape[0]
    tiles = state.shape[1]

    def slab(t, outward):
        near, far = post.at[:, t * N:(t + 1) * N], (post_out if outward else state).at[:, t, :]
        return pltpu.make_async_copy(near if outward else far, far if outward else near, state_sem.at[t])
    for t in range(tiles):
        slab(t, False).start()
    lanes = lax.broadcasted_iota(jnp.int32, (N, N), 1)
    eye = lanes == lax.broadcasted_iota(jnp.int32, (N, N), 0)
    member = lanes < M
    for b in range(batches):
        cur[b] = mats[b * (b + 1) // 2]

    def column(row):
        return jnp.sum(jnp.where(eye, row, 0.0), axis=1, keepdims=True)

    def batch(b, _):
        p = cur[b]
        avg = jnp.sum(jnp.where(member, p, 0.0), axis=1, keepdims=True) / M
        dev = jnp.where(member, p - avg, 0.0)
        var_row = variance[pl.ds(b, 1), :]
        var_col = column(var_row)
        obs_col = column(observed[pl.ds(b, 1), :])
        cov = dot(dev, dev, 1, 1) / (M - 1.0)
        work[:, 0:N] = jnp.where(eye, cov + var_row, cov)
        work[:, N:2 * N] = jnp.where(eye, 1.0, 0.0)
        work[:, 2 * N:3 * N] = jnp.where(lanes == M, obs_col - avg, dev)
        eliminate(work, solved, jnp.sqrt(var_col))
        a = solved[:, 0:N]
        m = solved[:, N:2 * N]
        t = dot(a, m, 0, 0)
        sinv = dot(a, a, 0, 0)
        gain = t - dot(sinv, var_col * t)
        incs[b] = dot(t, cov, 0, 1)[:M]

        def later(c, _):
            q = cur[c]
            g = dot(q, dev, 1, 1) * mats[c * (c + 1) // 2 + 1 + b] * (1.0 / (M - 1.0))
            cur[c] = q + dot(g, gain)
            return 0
        lax.fori_loop(b + 1, batches, later, 0)

        dev_m = dev[:, :M]
        gain_m = gain[:, :M]
        dh = dev_m.astype(bf16); dl = (dev_m - dh.astype(f32)).astype(bf16)
        dcat = jnp.concatenate([dh, dl, dh], axis=1)
        gt = gain.T[:M] * (1.0 / (M - 1.0))
        gh = gt.astype(bf16); gl = (gt - gh.astype(f32)).astype(bf16)
        gcat = jnp.concatenate([gh, gl, gh], axis=1)
        weights = local_w[b].T
        @pl.when(b == 0)
        def _():
            for t in range(tiles):
                slab(t, False).wait()
        for chunk in range(8):
            cs = 512 * chunk
            x = post[:, cs:cs + 512]
            xh = x.astype(bf16); xl = (x - xh.astype(f32)).astype(bf16)
            xcat = jnp.concatenate([xh, xh, xl], axis=0)
            r = dot(dcat, xcat, precision=None)
            scale = jnp.concatenate([jnp.broadcast_to(weights[:, t:t + 1], (N, N)) for t in range(4 * chunk, 4 * chunk + 4)], axis=1)
            r = r * scale
            rh = r.astype(bf16); rl = (r - rh.astype(f32)).astype(bf16)
            rcat = jnp.concatenate([rh, rh, rl], axis=0)
            post[:, cs:cs + 512] = x + dot(gcat, rcat, precision=None)
        return 0
    lax.fori_loop(0, batches, batch, 0)
    for t in range(tiles):
        slab(t, True).start()
    for t in range(tiles):
        slab(t, True).wait()

def chain(mats, observed, variance, state, local_w):
    batches = observed.shape[0]
    vm = pl.BlockSpec(memory_space=pltpu.VMEM)
    return pl.pallas_call(chain_kernel,
        out_shape=(jax.ShapeDtypeStruct(state.shape, f32), jax.ShapeDtypeStruct((batches, M, N), f32)),
        in_specs=[vm] * 3 + [pl.BlockSpec(memory_space=pl.ANY), vm], out_specs=(pl.BlockSpec(memory_space=pl.ANY), vm),
        scratch_shapes=[pltpu.VMEM((N, 3 * N), f32), pltpu.VMEM((N, 2 * N), f32), pltpu.VMEM((batches, N, N), f32),
            pltpu.VMEM((M, state.shape[1] * N), f32), pltpu.SemaphoreType.DMA((state.shape[1],))],
        compiler_params=pltpu.CompilerParams(vmem_limit_bytes=48 << 20),
        cost_estimate=pl.CostEstimate(flops=10**9, bytes_accessed=4 * 10**6, transcendentals=0),
    )(mats, observed, variance, state, local_w)


def local(prior_state, localization, observed, error_variance, owner_ids, obs_cell):
    members, _, cells = prior_state.shape
    tiles = cells // TILE
    batches = obs_cell.shape[0]
    weights = jnp.transpose(localization.reshape(batches, N, tiles), (0, 2, 1))
    send = extract(obs_cell, prior_state.reshape(members * tiles, TILE), weights)
    mats = share(owner_ids, send)
    state, increments = chain(mats, observed, error_variance, prior_state.reshape(members, tiles, TILE), weights)
    return state.reshape(members, 1, cells), jnp.transpose(increments, (0, 2, 1))


def solution(mesh):
    in_specs = (P(None, "lev", "horiz"), P(None, None, "lev", "horiz"), P(), P(), P(), P())
    out_specs = (P(None, "lev", "horiz"), P())
    return jax.shard_map(local, mesh=mesh, in_specs=in_specs, out_specs=out_specs, check_vma=False)
```

```python
import jax
import jax.numpy as jnp
from jax import lax
from jax.experimental import pallas as pl
from jax.experimental.pallas import tpu as pltpu
from jax.sharding import PartitionSpec as P

f32 = jnp.float32
bf16 = jnp.bfloat16
HI = lax.Precision.HIGHEST
MESH = pl.DeviceIdType.MESH
X_DIM, Z_DIM, Y_DIM = 4, 8, 8
TILE = 128
N, M = 128, 80
PER_LEVEL = N // Y_DIM


def dot(a, b, ca=1, cb=0, precision=HI):
    return lax.dot_general(a, b, (((ca,), (cb,)), ((), ())), precision=precision, preferred_element_type=f32)


def split3(x):
    h = x.astype(bf16).astype(f32)
    r = x - h
    m = r.astype(bf16).astype(f32)
    return h, m, r - m


def panel_product(left, right):
    h, m, l = split3(left)
    lhs = jnp.concatenate([h, h, m, m, h, l], axis=0).T.astype(bf16)
    h, m, l = split3(right)
    rhs = jnp.concatenate([h, m, h, m, l, h], axis=0).astype(bf16)
    return lax.dot_general(lhs, rhs, (((1,), (0,)), ((), ())), preferred_element_type=f32)


def eliminate(work, solved, root_col):
    row16 = lax.broadcasted_iota(jnp.int32, (16, N), 0)
    row8 = lax.broadcasted_iota(jnp.int32, (8, N), 0)
    lane1 = lax.broadcasted_iota(jnp.int32, (1, N), 1)
    for block in range(N // 8):
        r0 = 8 * block
        tall = 16 if block < N // 8 - 1 else 8
        rows = row16[:tall]
        win_s = work[r0:r0 + tall, 0:N]
        win_a = work[r0:r0 + tall, N:2 * N]
        win_d = work[r0:r0 + tall, 2 * N:3 * N]
        roots = jnp.broadcast_to(root_col[r0:r0 + 8, :], (8, N))
        cols = [jnp.broadcast_to(win_s[:, r0 + k:r0 + k + 1], (tall, N)) for k in range(8)]
        diag = jnp.ones((8, N), f32)
        used_d = jnp.zeros((8, N), f32)
        for j in range(8):
            d = cols[j][j:j + 1, :]
            g = jnp.where(rows > j, cols[j] * (1.0 / d), 0.0)
            for k in range(j + 1, 8):
                cols[k] = cols[k] - g * cols[k][j:j + 1, :]
            win_s = win_s - g * win_s[j:j + 1, :]
            win_a = win_a - g * win_a[j:j + 1, :]
            f = jnp.sqrt(d)
            s = jnp.where(lane1 < M, f / (f + roots[j:j + 1, :]), 1.0)
            scaled = win_d[j:j + 1, :] * s
            win_d = win_d - g * scaled
            diag = jnp.where(row8 == j, d, diag)
            used_d = jnp.where(row8 == j, scaled, used_d)
        if block < N // 8 - 1:
            work[r0 + 8:r0 + 16, 0:N] = win_s[8:]
            work[r0 + 8:r0 + 16, N:2 * N] = win_a[8:]
            work[r0 + 8:r0 + 16, 2 * N:3 * N] = win_d[8:]
        inv = lax.rsqrt(diag)
        f = diag * inv
        solved[r0:r0 + 8, 0:N] = win_a[:8] * inv
        v = jnp.broadcast_to(win_d[:8, M:M + 1], (8, N)) * inv
        solved[r0:r0 + 8, N:2 * N] = jnp.where(lane1 < M, v - win_d[:8] / (f + roots), 0.0)
        if r0 + 16 < N:
            right = jnp.concatenate([win_s[:8], win_a[:8], used_d], axis=1)
            update = panel_product(win_s[:8] / diag, right)
            work[r0 + 16:, :] = work[r0 + 16:, :] - update[r0 + 16:, :]


def first(b):
    return b * (b + 1) // 2


def rank(x, z, core):
    return (x * Z_DIM + z) * 2 + core


def kernel(owner_ids, send, observed, variance, state, weights, post_out, incs, *scratch):
    batches = observed.shape[0]
    tiles = state.shape[1]
    near = scratch[0:batches]
    line = scratch[batches:2 * batches]
    picked = scratch[2 * batches:3 * batches]
    mats, cur, devs, gains, work, solved, post, local_w, state_sem, weight_sem, push, arrive = scratch[3 * batches:]
    h, lev = lax.axis_index("horiz"), lax.axis_index("lev")
    x, z, core = h // (2 * Z_DIM), (h // 2) % Z_DIM, h % 2
    lanes = lax.broadcasted_iota(jnp.int32, (N, N), 1)
    eye = lanes == lax.broadcasted_iota(jnp.int32, (N, N), 0)
    member = lanes < M

    near_peers = [rank((x + s) % X_DIM, z, (core + c) % 2) for s in range(X_DIM) for c in range(2) if s or c]
    near_peers = [{"horiz": to, "lev": lev} for to in near_peers]
    line_peers = [{"horiz": rank(x, (z + s) % Z_DIM, core), "lev": lev} for s in range(1, Z_DIM)]
    level_peers = [{"horiz": h, "lev": (lev + s) % Y_DIM} for s in range(1, Y_DIM)]
    peers = [near_peers, line_peers, level_peers]

    barrier = pltpu.get_barrier_semaphore()
    for to in near_peers + line_peers + level_peers:
        pl.semaphore_signal(barrier, inc=1, device_id=to, device_id_type=MESH)

    def slab(t, outward):
        inside, far = post.at[:, t * N:(t + 1) * N], (post_out if outward else state).at[:, t, :]
        return pltpu.make_async_copy(inside if outward else far, far if outward else inside, state_sem.at[t])
    for t in range(tiles):
        slab(t, False).start()
    fetch = pltpu.make_async_copy(weights, local_w, weight_sem)
    fetch.start()
    def copies(b, stage):
        if stage == 0:
            source, target = send.at[first(b):first(b + 1)], near[b].at[x * 2 + core]
        elif stage == 1:
            source, target = picked[b], line[b].at[z]
        else:
            source, target = line[b].at[Z_DIM], mats.at[first(b):first(b + 1), lev]
        return [
            pltpu.make_async_remote_copy(source, target, push.at[b, stage, i], arrive.at[b, stage], device_id=to, device_id_type=MESH)
            for i, to in enumerate(peers[stage])
        ]

    def start(b, stage):
        owner = owner_ids[b]
        if stage == 0:
            near[b][x * 2 + core] = send[first(b):first(b + 1)]
        elif stage == 1:
            block = near[b][(owner // (2 * Z_DIM)) * 2 + owner % 2]
            picked[b][...] = block
            line[b][z] = block
        else:
            block = line[b][(owner // 2) % Z_DIM]
            line[b][Z_DIM] = block
            mats[first(b):first(b + 1), lev] = block
        for copy in copies(b, stage):
            copy.start()

    def arrived(b, stage):
        count = len(peers[stage])
        whole = [near[b].at[0:count], line[b].at[0:count], mats.at[first(b):first(b + 1), 0:count]][stage]
        pltpu.make_async_copy(whole, whole, arrive.at[b, stage]).wait()

    pl.semaphore_wait(barrier, len(near_peers) + len(line_peers) + len(level_peers))
    start(0, 0)
    start(1, 0)
    arrived(0, 0)
    start(0, 1)
    arrived(1, 0)
    start(1, 1)
    start(2, 0)
    arrived(0, 1)
    start(0, 2)
    arrived(1, 1)
    start(1, 2)
    arrived(2, 0)
    start(2, 1)
    start(3, 0)
    arrived(0, 2)

    for t in range(tiles):
        slab(t, False).wait()
    fetch.wait()

    def service(b):
        if b + 2 < batches:
            arrived(b + 2, 1)
            start(b + 2, 2)
        if b + 3 < batches:
            arrived(b + 3, 0)
            start(b + 3, 1)
        if b + 4 < batches:
            start(b + 4, 0)

    def column(row):
        return jnp.sum(jnp.where(eye, row, 0.0), axis=1, keepdims=True)

    def carry_over(c, a):
        q = cur[c]
        g = dot(q, devs[a], 1, 1) * mats[c * (c + 1) // 2 + 1 + a].reshape(N, N) * (1.0 / (M - 1.0))
        cur[c] = q + dot(g, gains[a])

    cur[0] = mats[0].reshape(N, N)

    def batch(b, _):
        p = cur[b]
        avg = jnp.sum(jnp.where(member, p, 0.0), axis=1, keepdims=True) / M
        dev = jnp.where(member, p - avg, 0.0)
        devs[b] = dev
        var_row = variance[pl.ds(b, 1), :]
        var_col = column(var_row)
        obs_col = column(observed[pl.ds(b, 1), :])
        cov = dot(dev, dev, 1, 1) / (M - 1.0)
        work[:, 0:N] = jnp.where(eye, cov + var_row, cov)
        work[:, N:2 * N] = jnp.where(eye, 1.0, 0.0)
        work[:, 2 * N:3 * N] = jnp.where(lanes == M, obs_col - avg, dev)
        eliminate(work, solved, jnp.sqrt(var_col))
        for k in range(batches):
            @pl.when(b == k)
            def _():
                service(k)
        a = solved[:, 0:N]
        m = solved[:, N:2 * N]
        t = dot(a, m, 0, 0)
        sinv = dot(a, a, 0, 0)
        gain = t - dot(sinv, var_col * t)
        gains[b] = gain
        incs[b] = dot(t, cov, 0, 1)[:M]

        for k in range(batches - 1):
            @pl.when(b == k)
            def _():
                arrived(k + 1, 2)
                cur[k + 1] = mats[first(k + 1)].reshape(N, N)

        @pl.when(b < batches - 1)
        def _():
            def past(a, _):
                carry_over(b + 1, a)
                return 0
            lax.fori_loop(0, b + 1, past, 0)

        dev_m = dev[:, :M]
        dh = dev_m.astype(bf16)
        dl = (dev_m - dh.astype(f32)).astype(bf16)
        dcat = jnp.concatenate([dh, dl, dh], axis=1)
        gt = gain.T[:M] * (1.0 / (M - 1.0))
        gh = gt.astype(bf16)
        gl = (gt - gh.astype(f32)).astype(bf16)
        gcat = jnp.concatenate([gh, gl, gh], axis=1)
        scales = local_w[b].T
        for chunk in range(tiles // 4):
            cs = 512 * chunk
            old = post[:, cs:cs + 512]
            xh = old.astype(bf16)
            xl = (old - xh.astype(f32)).astype(bf16)
            r = dot(dcat, jnp.concatenate([xh, xh, xl], axis=0), precision=None)
            scale = [jnp.broadcast_to(scales[:, t:t + 1], (N, N)) for t in range(4 * chunk, 4 * chunk + 4)]
            r = r * jnp.concatenate(scale, axis=1)
            rh = r.astype(bf16)
            rl = (r - rh.astype(f32)).astype(bf16)
            post[:, cs:cs + 512] = old + dot(gcat, jnp.concatenate([rh, rh, rl], axis=0), precision=None)
        return 0
    lax.fori_loop(0, batches, batch, 0)

    for t in range(tiles):
        slab(t, True).start()
    for b in range(batches):
        for stage in range(3):
            for copy in copies(b, stage):
                copy.wait_send()
    for t in range(tiles):
        slab(t, True).wait()


def extract_kernel(obs_cell, state, weights, send):
    batches, tiles = weights.shape[0], weights.shape[1]
    lev = lax.axis_index("lev")
    lane = lax.broadcasted_iota(jnp.int32, (M, N), 1)
    for b in range(batches):
        gathered = jnp.zeros((M, N), f32)
        for j in range(PER_LEVEL):
            cell = obs_cell[b, lev * PER_LEVEL + j]
            tile, at = cell // TILE, cell % TILE
            chunk = state[pl.ds(tile, M, stride=tiles), :]
            gathered = jnp.where(lane == j, pltpu.roll(chunk, lax.rem(j - at + N, N), 1), gathered)
            for a in range(b):
                send[first(b) + 1 + a, j:j + 1, :] = weights[a, pl.ds(tile, 1), :]
        square = jnp.concatenate([gathered, jnp.zeros((N - M, N), f32)], axis=0)
        send[first(b)] = square.T[:PER_LEVEL]


def extract(obs_cell, state, weights):
    vm = pl.BlockSpec(memory_space=pltpu.VMEM)
    return pl.pallas_call(
        extract_kernel,
        out_shape=jax.ShapeDtypeStruct((first(obs_cell.shape[0]), PER_LEVEL, N), f32),
        in_specs=[pl.BlockSpec(memory_space=pltpu.SMEM), vm, vm],
        out_specs=vm,
        compiler_params=pltpu.CompilerParams(vmem_limit_bytes=48 << 20),
    )(obs_cell, state, weights)


def assimilate(owner_ids, send, observed, variance, state, weights):
    batches = observed.shape[0]
    tiles = state.shape[1]
    vm = pl.BlockSpec(memory_space=pltpu.VMEM)
    smem = pl.BlockSpec(memory_space=pltpu.SMEM)
    hbm = pl.BlockSpec(memory_space=pl.ANY)
    dma = pltpu.SemaphoreType.DMA

    def block(*lead):
        return pltpu.VMEM((*lead, N), f32)
    count = first(batches)
    groups = [(b + 1, PER_LEVEL) for b in range(batches)]
    return pl.pallas_call(
        kernel,
        out_shape=(jax.ShapeDtypeStruct(state.shape, f32), jax.ShapeDtypeStruct((batches, M, N), f32)),
        in_specs=[smem, vm, vm, vm, hbm, hbm],
        out_specs=(hbm, vm),
        scratch_shapes=[block(2 * X_DIM, *g) for g in groups] + [block(Z_DIM + 1, *g) for g in groups] + [block(*g) for g in groups] + [
            block(count, Y_DIM, PER_LEVEL), block(batches, N), block(batches, N), block(batches, N),
            pltpu.VMEM((N, 3 * N), f32), pltpu.VMEM((N, 2 * N), f32), pltpu.VMEM((M, tiles * N), f32), block(batches, tiles),
            dma((tiles,)), dma, dma((batches, 3, max(2 * X_DIM, Z_DIM, Y_DIM) - 1)), dma((batches, 3)),
        ],
        compiler_params=pltpu.CompilerParams(vmem_limit_bytes=48 << 20, collective_id=0, has_side_effects=True),
        cost_estimate=pl.CostEstimate(flops=10**9, bytes_accessed=4 * 10**6, transcendentals=0),
    )(owner_ids, send, observed, variance, state, weights)


def local(prior_state, localization, observed, error_variance, owner_ids, obs_cell):
    members, _, cells = prior_state.shape
    tiles = cells // TILE
    batches = obs_cell.shape[0]
    weights = jnp.transpose(localization.reshape(batches, N, tiles), (0, 2, 1))
    send = extract(obs_cell, prior_state.reshape(members * tiles, TILE), weights)
    state, increments = assimilate(owner_ids, send, observed, error_variance, prior_state.reshape(members, tiles, TILE), weights)
    return state.reshape(members, 1, cells), jnp.transpose(increments, (0, 2, 1))


def solution(mesh):
    in_specs = (P(None, "lev", "horiz"), P(None, None, "lev", "horiz"), P(), P(), P(), P())
    out_specs = (P(None, "lev", "horiz"), P())
    return jax.shard_map(local, mesh=mesh, in_specs=in_specs, out_specs=out_specs, check_vma=False)
```

```python
import jax
import jax.numpy as jnp
from jax import lax
from jax.experimental import pallas as pl
from jax.experimental.pallas import tpu as pltpu
from jax.sharding import PartitionSpec as P

f32 = jnp.float32
bf16 = jnp.bfloat16
HI = lax.Precision.HIGHEST
MESH = pl.DeviceIdType.MESH
X_DIM, Z_DIM, Y_DIM = 4, 8, 8
TILE = 128
N, M = 128, 80
PER_LEVEL = N // Y_DIM
WHOLE_GROUPS = 2
ARRIVAL = (7, 5, 3, 3, 3)
SERVICES = {
    0: {0: [(3, 1)], 4: [(2, 2), (5, 0), (4, 1)]},
    1: {0: [(3, 2), (5, 1)], 3: [(2, 3)], 4: [(4, 2)], 7: [(3, 3)]},
    2: {0: [(5, 2)], 4: [(4, 3)]},
    3: {1: [(5, 3)]},
}


def dot(a, b, ca=1, cb=0, precision=HI):
    return lax.dot_general(a, b, (((ca,), (cb,)), ((), ())), precision=precision, preferred_element_type=f32)


def split3(x):
    h = x.astype(bf16).astype(f32)
    r = x - h
    m = r.astype(bf16).astype(f32)
    return h, m, r - m


def panel_product(left, right):
    h, m, l = split3(left)
    lhs = jnp.concatenate([h, h, m, m, h, l], axis=0).T.astype(bf16)
    h, m, l = split3(right)
    rhs = jnp.concatenate([h, m, h, m, l, h], axis=0).astype(bf16)
    return lax.dot_general(lhs, rhs, (((1,), (0,)), ((), ())), preferred_element_type=f32)


BLOCK = 16


def lane_copy(tile, lane):
    return jnp.take_along_axis(tile, jnp.full(tile.shape, lane, jnp.int32), axis=1)


def row_copy(tile, row):
    return jnp.broadcast_to(tile[row:row + 1], tile.shape)


def eliminate(work, sums, root_col, beside):
    row8 = lax.broadcasted_iota(jnp.int32, (8, N), 0)
    lane8 = lax.broadcasted_iota(jnp.int32, (8, N), 1)
    own = BLOCK // 8
    for r0 in range(0, N, BLOCK):
        tall = min(2 * BLOCK, N - r0) // 8
        inside = (lane8 >= r0) & (lane8 < r0 + BLOCK)
        win_s = [work[r0 + 8 * t:r0 + 8 * t + 8, 0:N] for t in range(tall)]
        win_d = [work[r0 + 8 * t:r0 + 8 * t + 8, N:2 * N] for t in range(tall)]
        roots = [jnp.broadcast_to(root_col[r0 + 8 * t:r0 + 8 * t + 8, :], (8, N)) for t in range(own)]
        cols = [[lane_copy(w, r0 + k) for w in win_s] for k in range(BLOCK)]
        win_s = [jnp.where(inside, jnp.where(lane8 == row8 + (r0 + 8 * t), 1.0, 0.0) if t < own else 0.0, w) for t, w in enumerate(win_s)]
        diag = [jnp.ones((8, N), f32)] * own
        unit = []
        for j in range(0, BLOCK, 2):
            i = j + 1
            home, sj, si = j // 8, j % 8, j % 8 + 1
            cj, ci = cols[j], cols[i]
            a, b, e = row_copy(cj[home], sj), row_copy(cj[home], si), row_copy(ci[home], si)
            det = a * e - b * b
            idet = 1.0 / det
            p, q, r = e * idet, b * idet, a * idet
            ia = 1.0 / a
            ratio = b * ia
            diag[home] = jnp.where(row8 == sj, a, jnp.where(row8 == si, det * ia, diag[home]))
            row_sj, row_si = row_copy(win_s[home], sj), row_copy(win_s[home], si)
            cols_j = {k: row_copy(cols[k][home], sj) for k in range(i + 1, BLOCK)}
            cols_i = {k: row_copy(cols[k][home], si) for k in range(i + 1, BLOCK)}
            unit_j, unit_i = {}, {}
            for t in range(home, tall):
                gj = cj[t] * p - ci[t] * q
                gi = ci[t] * r - cj[t] * q
                gd = cj[t] * ia
                if t == home:
                    below = row8 > si
                    gj, gi = jnp.where(below, gj, 0.0), jnp.where(below, gi, 0.0)
                    gd = jnp.where(row8 > sj, gd, 0.0)
                unit_j[t], unit_i[t] = gd, gi
                if not (t == home and si == 7):
                    for k in range(i + 1, BLOCK):
                        cols[k][t] = cols[k][t] - gj * cols_j[k] - gi * cols_i[k]
                if t == home:
                    gj = jnp.where(row8 == si, ratio, gj)
                win_s[t] = win_s[t] - gj * row_sj - gi * row_si
            unit += [unit_j, unit_i]
        inv = [lax.rsqrt(d) for d in diag]
        f = [d * v for d, v in zip(diag, inv)]
        shrink = [jnp.where(lane8 < M, f[t] / (f[t] + roots[t]), 1.0) for t in range(own)]
        for j in range(BLOCK):
            home = j // 8
            scaled = row_copy(win_d[home] * shrink[home], j % 8)
            for t in unit[j]:
                win_d[t] = win_d[t] - unit[j][t] * scaled
        for t in range(own, tall):
            work[r0 + 8 * t:r0 + 8 * t + 8, 0:N] = win_s[t]
            work[r0 + 8 * t:r0 + 8 * t + 8, N:2 * N] = win_d[t]
        block_s = jnp.concatenate(win_s[:own], axis=0)
        low = r0 + 2 * BLOCK
        if low < N:
            left = jnp.concatenate([win_s[t] / diag[t] for t in range(own)], axis=0)
            right = jnp.concatenate([block_s, jnp.concatenate([win_d[t] * shrink[t] for t in range(own)], axis=0)], axis=1)
            update = panel_product(left, right)
            old = work[low:, 0:N]
            gone = lax.broadcasted_iota(jnp.int32, old.shape, 1)
            work[low:, 0:N] = jnp.where((gone >= r0) & (gone < r0 + BLOCK), 0.0, old) - update[low:, 0:N]
            work[low:, N:2 * N] = work[low:, N:2 * N] - update[low:, N:2 * N]
        a = jnp.concatenate([jnp.where(lane8 < r0 + BLOCK, win_s[t] * inv[t], 0.0) for t in range(own)], axis=0)
        m = jnp.concatenate([win_d[t] * jnp.where(lane8 < M, -1.0 / (f[t] + roots[t]), inv[t]) for t in range(own)], axis=0)
        update = panel_product(a, jnp.concatenate([a, m], axis=1))
        if r0 == 0:
            sums[...] = update
        else:
            sums[0:r0 + BLOCK, :] = sums[0:r0 + BLOCK, :] + update[0:r0 + BLOCK]
        beside(r0 // BLOCK)


def first(b):
    return b * (b + 1) // 2


def rank(x, z, core):
    return (x * Z_DIM + z) * 2 + core


def kernel(owner_ids, send, observed, variance, state, weights, post_out, incs, *scratch):
    batches = observed.shape[0]
    tiles = state.shape[1]
    near = scratch[0:batches]
    line = scratch[batches:2 * batches]
    picked = scratch[2 * batches:3 * batches]
    (mats, cur, covs, devs, gains, terms, links, work, sums, post, local_w,
        state_sem, weight_sem, push, here) = scratch[3 * batches:]
    h, lev = lax.axis_index("horiz"), lax.axis_index("lev")
    x, z, core = h // (2 * Z_DIM), (h // 2) % Z_DIM, h % 2
    lanes = lax.broadcasted_iota(jnp.int32, (N, N), 1)
    eye = lanes == lax.broadcasted_iota(jnp.int32, (N, N), 0)
    member = lanes < M

    near_peers = [rank((x + s) % X_DIM, z, (core + c) % 2) for s in range(X_DIM) for c in range(2) if s or c]
    near_peers = [{"horiz": to, "lev": lev} for to in near_peers]
    line_peers = [{"horiz": rank(x, (z + s) % Z_DIM, core), "lev": lev} for s in range(1, Z_DIM)]
    level_peers = [{"horiz": h, "lev": (lev + s) % Y_DIM} for s in range(1, Y_DIM)]
    peers = [near_peers, line_peers, level_peers, [{"horiz": rank(x, z, 1 - core), "lev": lev}]]

    barrier = pltpu.get_barrier_semaphore()
    for to in near_peers + line_peers + level_peers:
        pl.semaphore_signal(barrier, inc=1, device_id=to, device_id_type=MESH)

    def slab(t, outward):
        inside, far = post.at[:, t * N:(t + 1) * N], (post_out if outward else state).at[:, t, :]
        return pltpu.make_async_copy(inside if outward else far, far if outward else inside, state_sem.at[t])
    fetch = pltpu.make_async_copy(weights, local_w, weight_sem)

    def shared(b):
        return b >= WHOLE_GROUPS

    def half(b, which):
        rows = PER_LEVEL // 2
        return pl.ds(pl.multiple_of(which * rows, rows), rows) if shared(b) else slice(None)

    def group(b):
        return slice(first(b), first(b + 1))

    def copies(b, stage):
        if stage == 0:
            source, target = send.at[group(b)], near[b].at[x * 2 + core]
        elif stage == 1:
            source, target = picked[b].at[:, half(b, core)], line[b].at[z]
        elif stage == 2:
            source, target = line[b].at[Z_DIM], mats.at[group(b), lev, half(b, core)]
        else:
            source = target = mats.at[group(b), :, half(b, core)]
        return [
            pltpu.make_async_remote_copy(source, target, push.at[b, stage, i], here.at[b, stage], device_id=to, device_id_type=MESH)
            for i, to in enumerate(peers[stage])
        ]

    def start(b, stage):
        owner = owner_ids[b]
        if stage == 0:
            near[b][x * 2 + core] = send[group(b)]
        elif stage == 1:
            picked[b][...] = near[b][(owner // (2 * Z_DIM)) * 2 + owner % 2]
            line[b][z] = picked[b][:, half(b, core)]
        elif stage == 2:
            block = line[b][(owner // 2) % Z_DIM]
            line[b][Z_DIM] = block
            mats[group(b), lev, half(b, core)] = block
        for copy in copies(b, stage):
            copy.start()

    def arrived(b, stage):
        count = len(peers[stage])
        if stage < 2:
            whole = [near, line][stage][b].at[0:count]
        else:
            whole = mats.at[group(b), 0:count, half(b, core)] if stage == 2 else mats.at[group(b), :, half(b, 1 - core)]
        pltpu.make_async_copy(whole, whole, here.at[b, stage]).wait()

    def advance(b, stage):
        if b < batches:
            if stage > 0:
                arrived(b, stage - 1)
            start(b, stage)

    def arrive(c):
        arrived(c, 3 if shared(c) else 2)
        cur[c] = centred(mats[first(c)].reshape(N, N))

    def weight(c, a):
        return mats[first(c) + 1 + a].reshape(N, N)

    def column(row):
        return jnp.sum(jnp.where(eye, row, 0.0), axis=1, keepdims=True)

    def centred(priors):
        mean = jnp.sum(jnp.where(member, priors, 0.0), axis=1, keepdims=True) / M
        return jnp.where(member, priors - mean, jnp.where(lanes == M, mean, 0.0))

    def link(c, a):
        return dot(cur[c], devs[a], 1, 1) * weight(c, a) * (1.0 / (M - 1.0))

    def carry_over(c, a):
        cur[c] = cur[c] + dot(link(c, a), gains[a])

    def whole(split):
        return split + jnp.sum(jnp.where(lanes == M, split, 0.0), axis=1, keepdims=True)

    def halves(x):
        h = x.astype(bf16)
        return h, (x - h.astype(f32)).astype(bf16)

    def finish(b):
        held = {}

        def prepare():
            incs[b] = dot(whole(terms[b]), covs[b], 0, 1)[:M]
            dh, dl = halves(devs[b][:, :M])
            held["d"] = jnp.concatenate([dh, dl, dh], axis=1)
            gh, gl = halves(whole(gains[b]).T[:M] * (1.0 / (M - 1.0)))
            held["g"] = jnp.concatenate([gh, gl, gh], axis=1)
            held["w"] = local_w[b].T
        wide = tiles * BLOCK

        def part(index):
            cs = wide * index
            old = post[:, cs:cs + wide]
            xh, xl = halves(old)
            r = dot(held["d"], jnp.concatenate([xh, xh, xl], axis=0), precision=None)
            scale = [jnp.broadcast_to(held["w"][:, t:t + 1], (N, N)) for t in range(cs // N, (cs + wide) // N)]
            rh, rl = halves(r * jnp.concatenate(scale, axis=1))
            post[:, cs:cs + wide] = old + dot(held["g"], jnp.concatenate([rh, rh, rl], axis=0), precision=None)
        return [prepare] + [lambda index=index: part(index) for index in range(tiles * N // wide)]

    def batch(b, services):
        blocks = N // BLOCK
        share = [[] for _ in range(blocks)]
        if b > 0:
            for k, step in enumerate(finish(b - 1)):
                share[max(k - 1, 0)].append(step)
        if b + 1 < batches:
            at = ARRIVAL[b]
            share[at].append(lambda: arrive(b + 1))
            for a in range(b):
                share[min(at + a, blocks - 1)].append(lambda a=a: carry_over(b + 1, a))

            def last_link():
                links[b] = link(b + 1, b)
            share[min(at + b, blocks - 1)].append(last_link)

        def beside(block):
            for group_moved, stage in services.get(block, ()):
                advance(group_moved, stage)
            for step in share[block]:
                step()
        p = cur[b]
        devs[b] = jnp.where(member, p, 0.0)
        dev = devs[b]
        var_row = variance[b:b + 1, :]
        var_col = column(var_row)
        cov = dot(dev, dev, 1, 1) * (1.0 / (M - 1.0))
        covs[b] = cov
        work[:, 0:N] = jnp.where(eye, cov + var_row, cov)
        work[:, N:2 * N] = jnp.where(lanes == M, column(observed[b:b + 1, :]) - p, dev)
        eliminate(work, sums, jnp.sqrt(var_col), beside)
        t = sums[:, N:2 * N]
        terms[b] = t
        gain = t - dot(sums[:, 0:N], var_col * t)
        gains[b] = gain
        if b + 1 < batches:
            cur[b + 1] = cur[b + 1] + dot(links[b], gain)

    pl.semaphore_wait(barrier, len(near_peers) + len(line_peers) + len(level_peers))
    advance(0, 0)
    advance(1, 0)
    advance(2, 0)
    for t in range(tiles):
        slab(t, False).start()
    fetch.start()
    advance(0, 1)
    advance(1, 1)
    advance(3, 0)
    advance(0, 2)
    advance(2, 1)
    advance(1, 2)
    advance(4, 0)
    arrive(0)
    services = SERVICES
    for b in range(batches):
        if b == 1:
            for t in range(tiles):
                slab(t, False).wait()
            fetch.wait()
        batch(b, services.get(b, {}))
    for step in finish(batches - 1):
        step()

    for t in range(tiles):
        slab(t, True).start()
    for b in range(batches):
        for stage in range(4 if shared(b) else 3):
            for copy in copies(b, stage):
                copy.wait_send()
    for t in range(tiles):
        slab(t, True).wait()


def extract_kernel(obs_cell, state, weights, send):
    batches, tiles = weights.shape[0], weights.shape[1]
    lev = lax.axis_index("lev")
    lane = lax.broadcasted_iota(jnp.int32, (M, N), 1)
    for b in range(batches):
        gathered = jnp.zeros((M, N), f32)
        for j in range(PER_LEVEL):
            cell = obs_cell[b, lev * PER_LEVEL + j]
            tile, at = cell // TILE, cell % TILE
            chunk = state[pl.ds(tile, M, stride=tiles), :]
            gathered = jnp.where(lane == j, pltpu.roll(chunk, lax.rem(j - at + N, N), 1), gathered)
            for a in range(b):
                send[first(b) + 1 + a, j:j + 1, :] = weights[a, pl.ds(tile, 1), :]
        square = jnp.concatenate([gathered, jnp.zeros((N - M, N), f32)], axis=0)
        send[first(b)] = square.T[:PER_LEVEL]


def extract(obs_cell, state, weights):
    vm = pl.BlockSpec(memory_space=pltpu.VMEM)
    return pl.pallas_call(
        extract_kernel,
        out_shape=jax.ShapeDtypeStruct((first(obs_cell.shape[0]), PER_LEVEL, N), f32),
        in_specs=[pl.BlockSpec(memory_space=pltpu.SMEM), vm, vm],
        out_specs=vm,
        compiler_params=pltpu.CompilerParams(vmem_limit_bytes=48 << 20),
    )(obs_cell, state, weights)


def assimilate(owner_ids, send, observed, variance, state, weights):
    batches = observed.shape[0]
    tiles = state.shape[1]
    vm = pl.BlockSpec(memory_space=pltpu.VMEM)
    smem = pl.BlockSpec(memory_space=pltpu.SMEM)
    hbm = pl.BlockSpec(memory_space=pl.ANY)
    dma = pltpu.SemaphoreType.DMA

    def block(*lead):
        return pltpu.VMEM((*lead, N), f32)
    groups = [(b + 1, PER_LEVEL) for b in range(batches)]
    parts = [(b + 1, PER_LEVEL // (1 if b < WHOLE_GROUPS else 2)) for b in range(batches)]
    return pl.pallas_call(
        kernel,
        out_shape=(jax.ShapeDtypeStruct(state.shape, f32), jax.ShapeDtypeStruct((batches, M, N), f32)),
        in_specs=[smem, vm, vm, vm, hbm, hbm],
        out_specs=(hbm, vm),
        scratch_shapes=[block(2 * X_DIM, *g) for g in groups] + [block(Z_DIM + 1, *g) for g in parts] + [block(*g) for g in groups] + [
            block(first(batches), Y_DIM, PER_LEVEL)] + [block(batches, N)] * 6 + [
            pltpu.VMEM((N, 2 * N), f32), pltpu.VMEM((N, 2 * N), f32), pltpu.VMEM((M, tiles * N), f32), block(batches, tiles),
            dma((tiles,)), dma, dma((batches, 4, max(2 * X_DIM, Z_DIM, Y_DIM) - 1)), dma((batches, 4)),
        ],
        compiler_params=pltpu.CompilerParams(vmem_limit_bytes=48 << 20, collective_id=0, has_side_effects=True),
        cost_estimate=pl.CostEstimate(flops=10**9, bytes_accessed=4 * 10**6, transcendentals=0),
    )(owner_ids, send, observed, variance, state, weights)


def local(prior_state, localization, observed, error_variance, owner_ids, obs_cell):
    members, _, cells = prior_state.shape
    tiles = cells // TILE
    batches = obs_cell.shape[0]
    weights = jnp.transpose(localization.reshape(batches, N, tiles), (0, 2, 1))
    send = extract(obs_cell, prior_state.reshape(members * tiles, TILE), weights)
    state, increments = assimilate(owner_ids, send, observed, error_variance, prior_state.reshape(members, tiles, TILE), weights)
    return state.reshape(members, 1, cells), jnp.transpose(increments, (0, 2, 1))


def solution(mesh):
    in_specs = (P(None, "lev", "horiz"), P(None, None, "lev", "horiz"), P(), P(), P(), P())
    out_specs = (P(None, "lev", "horiz"), P())
    return jax.shard_map(local, mesh=mesh, in_specs=in_specs, out_specs=out_specs, check_vma=False)
```

```python
import jax
import jax.numpy as jnp
from jax import lax
from jax.experimental import pallas as pl
from jax.experimental.pallas import tpu as pltpu
from jax.sharding import PartitionSpec as P

f32 = jnp.float32
bf16 = jnp.bfloat16
HI = lax.Precision.HIGHEST
MESH = pl.DeviceIdType.MESH
X_DIM, Z_DIM, Y_DIM = 4, 8, 8
TILE = 128
N, M = 128, 80
PER_LEVEL = N // Y_DIM
WHOLE_GROUPS = 2
PLACES = (0, 0, 1, 2, 3, 4, 6, 8, 9)
ARRIVAL = (7, 5, 3, 3, 3)
SERVICES = {
    0: {0: [(3, 1)], 4: [(2, 2), (5, 0), (4, 1)]},
    1: {0: [(3, 2), (5, 1)], 3: [(2, 3)], 4: [(4, 2)], 7: [(3, 3)]},
    2: {0: [(5, 2)], 4: [(4, 3)]},
    3: {1: [(5, 3)]},
}


def dot(a, b, ca=1, cb=0, precision=HI):
    return lax.dot_general(a, b, (((ca,), (cb,)), ((), ())), precision=precision, preferred_element_type=f32)


def split3(x):
    h = x.astype(bf16).astype(f32)
    r = x - h
    m = r.astype(bf16).astype(f32)
    return h, m, r - m


def panel_product(left, right):
    h, m, l = split3(left)
    lhs = jnp.concatenate([h, h, m, m, h, l], axis=0).T.astype(bf16)
    h, m, l = split3(right)
    rhs = jnp.concatenate([h, m, h, m, l, h], axis=0).astype(bf16)
    return lax.dot_general(lhs, rhs, (((1,), (0,)), ((), ())), preferred_element_type=f32)


BLOCK = 16
AHEAD = 16
SUMMED = 32


def lane_copy(tile, lane):
    return jnp.take_along_axis(tile, jnp.full(tile.shape, lane, jnp.int32), axis=1)


def row_copy(tile, row):
    return jnp.broadcast_to(tile[row:row + 1], tile.shape)


def eliminate(work, sums, root_col, beside):
    row8 = lax.broadcasted_iota(jnp.int32, (8, N), 0)
    lane8 = lax.broadcasted_iota(jnp.int32, (8, N), 1)
    own = BLOCK // 8
    kept_a, kept_m = [], []
    for r0 in range(0, N, BLOCK):
        tall = min(BLOCK + AHEAD, N - r0) // 8
        inside = (lane8 >= r0) & (lane8 < r0 + BLOCK)
        win_s = [work[r0 + 8 * t:r0 + 8 * t + 8, 0:N] for t in range(tall)]
        win_d = [work[r0 + 8 * t:r0 + 8 * t + 8, N:2 * N] for t in range(tall)]
        roots = [jnp.broadcast_to(root_col[r0 + 8 * t:r0 + 8 * t + 8, :], (8, N)) for t in range(own)]
        cols = [[lane_copy(w, r0 + k) for w in win_s] for k in range(BLOCK)]
        win_s = [jnp.where(inside, jnp.where(lane8 == row8 + (r0 + 8 * t), 1.0, 0.0) if t < own else 0.0, w) for t, w in enumerate(win_s)]
        diag = [jnp.ones((8, N), f32)] * own
        unit = []
        for j in range(0, BLOCK, 2):
            i = j + 1
            home, sj, si = j // 8, j % 8, j % 8 + 1
            cj, ci = cols[j], cols[i]
            a, b, e = row_copy(cj[home], sj), row_copy(cj[home], si), row_copy(ci[home], si)
            det = a * e - b * b
            idet = 1.0 / det
            p, q, r = e * idet, b * idet, a * idet
            ia = 1.0 / a
            ratio = b * ia
            diag[home] = jnp.where(row8 == sj, a, jnp.where(row8 == si, det * ia, diag[home]))
            row_sj, row_si = row_copy(win_s[home], sj), row_copy(win_s[home], si)
            cols_j = {k: row_copy(cols[k][home], sj) for k in range(i + 1, BLOCK)}
            cols_i = {k: row_copy(cols[k][home], si) for k in range(i + 1, BLOCK)}
            unit_j, unit_i = {}, {}
            for t in range(home, tall):
                gj = cj[t] * p - ci[t] * q
                gi = ci[t] * r - cj[t] * q
                gd = cj[t] * ia
                if t == home:
                    below = row8 > si
                    gj, gi = jnp.where(below, gj, 0.0), jnp.where(below, gi, 0.0)
                    gd = jnp.where(row8 > sj, gd, 0.0)
                unit_j[t], unit_i[t] = gd, gi
                if not (t == home and si == 7):
                    for k in range(i + 1, BLOCK):
                        cols[k][t] = cols[k][t] - gj * cols_j[k] - gi * cols_i[k]
                if t == home:
                    gj = jnp.where(row8 == si, ratio, gj)
                win_s[t] = win_s[t] - gj * row_sj - gi * row_si
            unit += [unit_j, unit_i]
        inv = [lax.rsqrt(d) for d in diag]
        f = [d * v for d, v in zip(diag, inv)]
        shrink = [jnp.where(lane8 < M, f[t] / (f[t] + roots[t]), 1.0) for t in range(own)]
        for j in range(BLOCK):
            home = j // 8
            scaled = row_copy(win_d[home] * shrink[home], j % 8)
            for t in unit[j]:
                win_d[t] = win_d[t] - unit[j][t] * scaled
        for t in range(own, tall):
            work[r0 + 8 * t:r0 + 8 * t + 8, 0:N] = win_s[t]
            work[r0 + 8 * t:r0 + 8 * t + 8, N:2 * N] = win_d[t]
        block_s = jnp.concatenate(win_s[:own], axis=0)
        low = r0 + BLOCK + AHEAD
        if low < N:
            left = jnp.concatenate([win_s[t] / diag[t] for t in range(own)], axis=0)
            right = jnp.concatenate([block_s, jnp.concatenate([win_d[t] * shrink[t] for t in range(own)], axis=0)], axis=1)
            update = panel_product(left, right)
            old = work[low:, 0:N]
            gone = lax.broadcasted_iota(jnp.int32, old.shape, 1)
            work[low:, 0:N] = jnp.where((gone >= r0) & (gone < r0 + BLOCK), 0.0, old) - update[low:, 0:N]
            work[low:, N:2 * N] = work[low:, N:2 * N] - update[low:, N:2 * N]
        kept_a += [jnp.where(lane8 < r0 + BLOCK, win_s[t] * inv[t], 0.0) for t in range(own)]
        kept_m += [win_d[t] * jnp.where(lane8 < M, -1.0 / (f[t] + roots[t]), inv[t]) for t in range(own)]
        if len(kept_a) == SUMMED // 8:
            a, m = jnp.concatenate(kept_a, axis=0), jnp.concatenate(kept_m, axis=0)
            kept_a, kept_m = [], []
            update = panel_product(a, jnp.concatenate([a, m], axis=1))
            done = r0 + BLOCK
            if done == SUMMED:
                sums[...] = update
            else:
                sums[0:done, :] = sums[0:done, :] + update[0:done]
        beside(r0 // BLOCK)


def first(b):
    return b * (b + 1) // 2


def rank(x, z, core):
    return (x * Z_DIM + z) * 2 + core


def halves(x):
    h = x.astype(bf16)
    return h, (x - h.astype(f32)).astype(bf16)


def whole(split):
    lanes = lax.broadcasted_iota(jnp.int32, split.shape, 1)
    return split + jnp.sum(jnp.where(lanes == M, split, 0.0), axis=1, keepdims=True)


def finish(dev, gain, term, cov, weights, old, new, increments):
    cells = old.shape[1]
    held = {}

    def prepare():
        increments(dot(whole(term()), cov(), 0, 1)[:M])
        dh, dl = halves(dev()[:, :M])
        held["d"] = jnp.concatenate([dh, dl, dh], axis=1)
        gh, gl = halves(whole(gain()).T[:M] * (1.0 / (M - 1.0)))
        held["g"] = jnp.concatenate([gh, gl, gh], axis=1)
        held["w"] = weights().T
    wide = 4 * N

    def part(index):
        cs = wide * index
        x = old[:, cs:cs + wide]
        xh, xl = halves(x)
        r = dot(held["d"], jnp.concatenate([xh, xh, xl], axis=0), precision=None)
        scale = [jnp.broadcast_to(held["w"][:, t:t + 1], (N, N)) for t in range(cs // N, (cs + wide) // N)]
        rh, rl = halves(r * jnp.concatenate(scale, axis=1))
        new[:, cs:cs + wide] = x + dot(held["g"], jnp.concatenate([rh, rh, rl], axis=0), precision=None)
    return [prepare] + [lambda index=index: part(index) for index in range(cells // wide)]


def kernel(owner_ids, obs_cell, observed, variance, state, weights, post_out, incs, last, last_w, *scratch):
    batches = observed.shape[0]
    tiles = state.shape[1]
    near = scratch[0:batches]
    line = scratch[batches:2 * batches]
    picked = scratch[2 * batches:3 * batches]
    (send, mats, cur, covs, devs, gains, terms, links, work, sums, post, local_w,
        state_sem, weight_sem, push, here) = scratch[3 * batches:]
    h, lev = lax.axis_index("horiz"), lax.axis_index("lev")
    x, z, core = h // (2 * Z_DIM), (h // 2) % Z_DIM, h % 2
    lanes = lax.broadcasted_iota(jnp.int32, (N, N), 1)
    eye = lanes == lax.broadcasted_iota(jnp.int32, (N, N), 0)
    member = lanes < M

    near_peers = [rank((x + s) % X_DIM, z, (core + c) % 2) for s in range(X_DIM) for c in range(2) if s or c]
    near_peers = [{"horiz": to, "lev": lev} for to in near_peers]
    line_peers = [{"horiz": rank(x, (z + s) % Z_DIM, core), "lev": lev} for s in range(1, Z_DIM)]
    level_peers = [{"horiz": h, "lev": (lev + s) % Y_DIM} for s in range(1, Y_DIM)]
    peers = [near_peers, line_peers, level_peers, [{"horiz": rank(x, z, 1 - core), "lev": lev}]]

    barrier = pltpu.get_barrier_semaphore()
    for to in near_peers + line_peers + level_peers:
        pl.semaphore_signal(barrier, inc=1, device_id=to, device_id_type=MESH)

    def slab(t):
        return pltpu.make_async_copy(state.at[:, t, :], post.at[:, t * N:(t + 1) * N], state_sem.at[t])
    def onward(k):
        chunk = slice(4 * N * k, 4 * N * (k + 1))
        return pltpu.make_async_copy(post.at[:, chunk], post_out.at[:, chunk], state_sem.at[k])
    fetch = pltpu.make_async_copy(weights, local_w, weight_sem)

    def shared(b):
        return b >= WHOLE_GROUPS

    def half(b, which):
        rows = PER_LEVEL // 2
        return pl.ds(pl.multiple_of(which * rows, rows), rows) if shared(b) else slice(None)

    def group(b):
        return slice(first(b), first(b + 1))

    def copies(b, stage):
        if stage == 0:
            source, target = send.at[group(b)], near[b].at[x * 2 + core]
        elif stage == 1:
            source, target = picked[b].at[:, half(b, core)], line[b].at[z]
        elif stage == 2:
            source, target = line[b].at[Z_DIM], mats.at[group(b), lev, half(b, core)]
        else:
            source = target = mats.at[group(b), :, half(b, core)]
        return [
            pltpu.make_async_remote_copy(source, target, push.at[b, stage, i], here.at[b, stage], device_id=to, device_id_type=MESH)
            for i, to in enumerate(peers[stage])
        ]

    def start(b, stage):
        owner = owner_ids[b]
        if stage == 0:
            near[b][x * 2 + core] = send[group(b)]
        elif stage == 1:
            picked[b][...] = near[b][(owner // (2 * Z_DIM)) * 2 + owner % 2]
            line[b][z] = picked[b][:, half(b, core)]
        elif stage == 2:
            block = line[b][(owner // 2) % Z_DIM]
            line[b][Z_DIM] = block
            mats[group(b), lev, half(b, core)] = block
        for copy in copies(b, stage):
            copy.start()

    def arrived(b, stage):
        count = len(peers[stage])
        if stage < 2:
            whole = [near, line][stage][b].at[0:count]
        else:
            whole = mats.at[group(b), 0:count, half(b, core)] if stage == 2 else mats.at[group(b), :, half(b, 1 - core)]
        pltpu.make_async_copy(whole, whole, here.at[b, stage]).wait()

    def advance(b, stage):
        if b < batches:
            if stage > 0:
                arrived(b, stage - 1)
            start(b, stage)

    def arrive(c):
        arrived(c, 3 if shared(c) else 2)
        cur[c] = centred(mats[first(c)].reshape(N, N))

    def weight(c, a):
        return mats[first(c) + 1 + a].reshape(N, N)

    def column(row):
        return jnp.sum(jnp.where(eye, row, 0.0), axis=1, keepdims=True)

    def centred(priors):
        mean = jnp.sum(jnp.where(member, priors, 0.0), axis=1, keepdims=True) / M
        return jnp.where(member, priors - mean, jnp.where(lanes == M, mean, 0.0))

    def link(c, a):
        return dot(cur[c], devs[a], 1, 1) * weight(c, a) * (1.0 / (M - 1.0))

    def carry_over(c, a):
        cur[c] = cur[c] + dot(link(c, a), gains[a])

    def batch(b, services):
        blocks = N // BLOCK
        share = [[] for _ in range(blocks + 2)]
        if b > 0:
            def keep(value):
                incs[b - 1] = value
            before = finish(*[lambda ref=ref: ref[b - 1] for ref in (devs, gains, terms, covs, local_w)], post, post, keep)
            for k, step in enumerate(before):
                if b == batches - 1 and k > 0:
                    step = lambda k=k, step=step: (step(), onward(k - 1).start())
                share[PLACES[k]].append(step)
        if b + 1 < batches:
            at = ARRIVAL[b]
            share[at].append(lambda: arrive(b + 1))
            for a in range(b):
                share[min(at + a, blocks - 1)].append(lambda a=a: carry_over(b + 1, a))

            def last_link():
                links[b] = link(b + 1, b)
            share[min(at + b, blocks - 1)].append(last_link)

        def beside(block):
            for group_moved, stage in services.get(block, ()):
                advance(group_moved, stage)
            for step in share[block]:
                step()
        p = cur[b]
        devs[b] = jnp.where(member, p, 0.0)
        dev = devs[b]
        var_row = variance[b:b + 1, :]
        var_col = column(var_row)
        cov = dot(dev, dev, 1, 1) * (1.0 / (M - 1.0))
        covs[b] = cov
        work[:, 0:N] = jnp.where(eye, cov + var_row, cov)
        work[:, N:2 * N] = jnp.where(lanes == M, column(observed[b:b + 1, :]) - p, dev)
        eliminate(work, sums, jnp.sqrt(var_col), beside)
        t = sums[:, N:2 * N]
        terms[b] = t
        beside(blocks)
        gain = t - dot(sums[:, 0:N], var_col * t)
        gains[b] = gain
        beside(blocks + 1)
        if b + 1 < batches:
            cur[b + 1] = cur[b + 1] + dot(links[b], gain)

    for t in range(tiles):
        slab(t).start()
    fetch.start()
    row_lanes = lax.broadcasted_iota(jnp.int32, (8, N), 1)
    cells = jnp.zeros((8, N), jnp.int32)
    for b in range(batches):
        turned = pltpu.roll(jnp.broadcast_to(obs_cell[b:b + 1, :], (8, N)), (b * PER_LEVEL - lev * PER_LEVEL + N) % N, 1)
        cells = jnp.where((row_lanes >= b * PER_LEVEL) & (row_lanes < (b + 1) * PER_LEVEL), turned, cells)
    cells = cells[0:1]
    tile_of = column((cells // TILE).astype(f32))
    in_tile = jnp.where(lax.broadcasted_iota(jnp.int32, (N, tiles), 1).astype(f32) == tile_of, 1.0, 0.0)
    wide = 4 * N
    gathered = jnp.zeros((3 * M, N), f32)
    for cs in range(0, tiles * N, wide):
        for t in range(cs // N, (cs + wide) // N):
            slab(t).wait()
        parts = jnp.concatenate(split3(post[:, cs:cs + wide]), axis=0).astype(bf16)
        chosen = jnp.where(lax.broadcasted_iota(jnp.int32, (wide, N), 0) + cs == cells, 1.0, 0.0).astype(bf16)
        gathered = gathered + dot(parts, chosen, precision=None)
    gathered = gathered[:M] + gathered[M:2 * M] + gathered[2 * M:]
    rows = jnp.concatenate([gathered, jnp.zeros((N - M, N), f32)], axis=0).T
    for b in range(batches):
        send[first(b)] = rows[b * PER_LEVEL:(b + 1) * PER_LEVEL]
    pl.semaphore_wait(barrier, len(near_peers) + len(line_peers) + len(level_peers))
    advance(0, 0)
    fetch.wait()
    for a in range(batches - 1):
        rows = dot(in_tile, local_w[a])
        for b in range(a + 1, batches):
            send[first(b) + 1 + a] = rows[b * PER_LEVEL:(b + 1) * PER_LEVEL]
    advance(1, 0)
    advance(2, 0)
    advance(0, 1)
    advance(1, 1)
    advance(3, 0)
    advance(0, 2)
    advance(2, 1)
    advance(1, 2)
    advance(4, 0)
    arrive(0)
    services = SERVICES
    for b in range(batches):
        batch(b, services.get(b, {}))
    for k, ref in enumerate((devs, gains, terms, covs)):
        last[k] = ref[batches - 1]
    last_w[...] = local_w[batches - 1]
    for k in range(tiles // 4):
        onward(k).wait()
    for b in range(batches):
        for stage in range(4 if shared(b) else 3):
            for copy in copies(b, stage):
                copy.wait_send()


def last_kernel(slab, incs, factors, weights, state_out, incs_out, old, new, held, held_w, last_inc, state_sem, slab_sem, small_sem):
    batches = incs.shape[0]
    tiles = state_out.shape[1]

    def inward(k):
        chunk = slice(4 * N * k, 4 * N * (k + 1))
        return pltpu.make_async_copy(slab.at[:, chunk], old.at[:, chunk], slab_sem.at[k])

    def outward(t):
        return pltpu.make_async_copy(new.at[:, t * N:(t + 1) * N], state_out.at[:, t, :], state_sem.at[t])
    small = [
        pltpu.make_async_copy(factors, held, small_sem.at[0]),
        pltpu.make_async_copy(weights, held_w, small_sem.at[1]),
        pltpu.make_async_copy(incs.at[0:batches - 1], incs_out.at[0:batches - 1], small_sem.at[2]),
    ]
    own = pltpu.make_async_copy(last_inc, incs_out.at[batches - 1], small_sem.at[3])
    for copy in small[:2] + [inward(k) for k in range(tiles // 4)] + small[2:]:
        copy.start()

    def keep(value):
        last_inc[...] = value
    steps = finish(*[lambda k=k: held[k] for k in range(4)], lambda: held_w[...], old, new, keep)
    for copy in small[:2]:
        copy.wait()
    for k, step in enumerate(steps):
        if k == 0:
            step()
            own.start()
        else:
            inward(k - 1).wait()
            step()
            for t in range(4 * (k - 1), 4 * k):
                outward(t).start()
    small[2].wait()
    own.wait()
    for t in range(tiles):
        outward(t).wait()


def conclude(slab, incs, factors, weights, state_shape):
    hbm = pl.BlockSpec(memory_space=pltpu.MemorySpace.HBM)
    dma = pltpu.SemaphoreType.DMA
    return pl.pallas_call(
        last_kernel,
        out_shape=(jax.ShapeDtypeStruct(state_shape, f32), jax.ShapeDtypeStruct(incs.shape, f32)),
        in_specs=[hbm] * 4,
        out_specs=(hbm, hbm),
        scratch_shapes=[pltpu.VMEM(ref.shape, f32) for ref in (slab, slab, factors, weights)] + [
            pltpu.VMEM((M, N), f32), dma((state_shape[1],)), dma((state_shape[1] // 4,)), dma((4,)),
        ],
        compiler_params=pltpu.CompilerParams(vmem_limit_bytes=60 << 20),
    )(slab, incs, factors, weights)


def assimilate(owner_ids, obs_cell, observed, variance, state, weights):
    batches = observed.shape[0]
    tiles = state.shape[1]
    vm = pl.BlockSpec(memory_space=pltpu.VMEM)
    smem = pl.BlockSpec(memory_space=pltpu.SMEM)
    hbm = pl.BlockSpec(memory_space=pltpu.MemorySpace.HBM)
    dma = pltpu.SemaphoreType.DMA

    def block(*lead):
        return pltpu.VMEM((*lead, N), f32)
    groups = [(b + 1, PER_LEVEL) for b in range(batches)]
    parts = [(b + 1, PER_LEVEL // (1 if b < WHOLE_GROUPS else 2)) for b in range(batches)]
    return pl.pallas_call(
        kernel,
        out_shape=tuple(jax.ShapeDtypeStruct(shape, f32) for shape in (
            (M, tiles * N), (batches, M, N), (4, N, N), (tiles, N))),
        in_specs=[smem, vm, vm, vm, hbm, hbm],
        out_specs=(hbm, vm, vm, vm),
        scratch_shapes=[block(2 * X_DIM, *g) for g in groups] + [block(Z_DIM + 1, *g) for g in parts] + [block(*g) for g in groups] + [
            block(first(batches), PER_LEVEL), block(first(batches), Y_DIM, PER_LEVEL)] + [block(batches, N)] * 6 + [
            pltpu.VMEM((N, 2 * N), f32), pltpu.VMEM((N, 2 * N), f32), pltpu.VMEM((M, tiles * N), f32), block(batches, tiles),
            dma((tiles,)), dma, dma((batches, 4, max(2 * X_DIM, Z_DIM, Y_DIM) - 1)), dma((batches, 4)),
        ],
        compiler_params=pltpu.CompilerParams(vmem_limit_bytes=60 << 20, collective_id=0, has_side_effects=True),
        cost_estimate=pl.CostEstimate(flops=10**9, bytes_accessed=4 * 10**6, transcendentals=0),
    )(owner_ids, obs_cell, observed, variance, state, weights)


def local(prior_state, localization, observed, error_variance, owner_ids, obs_cell):
    members, _, cells = prior_state.shape
    tiles = cells // TILE
    batches = obs_cell.shape[0]
    weights = jnp.transpose(localization.reshape(batches, N, tiles), (0, 2, 1))
    state = prior_state.reshape(members, tiles, TILE)
    slab, increments, factors, last_weights = assimilate(owner_ids, obs_cell, observed, error_variance, state, weights)
    state, increments = conclude(slab, increments, factors, last_weights, state.shape)
    return state.reshape(members, 1, cells), jnp.transpose(increments, (0, 2, 1))


def solution(mesh):
    in_specs = (P(None, "lev", "horiz"), P(None, None, "lev", "horiz"), P(), P(), P(), P())
    out_specs = (P(None, "lev", "horiz"), P())
    return jax.shard_map(local, mesh=mesh, in_specs=in_specs, out_specs=out_specs, check_vma=False)
```

```python
import jax
import jax.numpy as jnp
from jax import lax
from jax.experimental import pallas as pl
from jax.experimental.pallas import tpu as pltpu
from jax.sharding import PartitionSpec as P

f32 = jnp.float32
bf16 = jnp.bfloat16
HI = lax.Precision.HIGHEST
MESH = pl.DeviceIdType.MESH
X_DIM, Z_DIM, Y_DIM = 4, 8, 8
TILE = 128
N, M = 128, 80
PER_LEVEL = N // Y_DIM
WHOLE_GROUPS = 2
GROUPED = 4
PLACES = (0, 0, 1, 2, 3, 4, 6, 8, 9)
ARRIVAL = (7, 5, 3, 3, 3)
SERVICES = {
    0: {0: [(3, 1)], 4: [(2, 2), (5, 0), (4, 1)]},
    1: {0: [(3, 2), (5, 1)], 3: [(2, 3)], 4: [(4, 2)], 7: [(3, 3)]},
    2: {0: [(5, 2)], 4: [(4, 3)]},
    3: {1: [(5, 3)]},
}


def dot(a, b, ca=1, cb=0, precision=HI):
    return lax.dot_general(a, b, (((ca,), (cb,)), ((), ())), precision=precision, preferred_element_type=f32)


def split3(x):
    h = x.astype(bf16).astype(f32)
    r = x - h
    m = r.astype(bf16).astype(f32)
    return h, m, r - m


def panel_product(left, right, rows):
    h, m, l = split3(left)
    lhs = jnp.concatenate([h, h, m, m, h, l], axis=0).T[rows].astype(bf16)
    h, m, l = split3(right)
    rhs = jnp.concatenate([h, m, h, m, l, h], axis=0).astype(bf16)
    return lax.dot_general(lhs, rhs, (((1,), (0,)), ((), ())), preferred_element_type=f32)


BLOCK = 16
AHEAD = 16
SUMMED = 16


def lane_copy(tile, lane):
    return jnp.take_along_axis(tile, jnp.full(tile.shape, lane, jnp.int32), axis=1)


def row_copy(tile, row):
    return jnp.broadcast_to(tile[row:row + 1], tile.shape)


def eliminate(work, sums, root_col, beside):
    row8 = lax.broadcasted_iota(jnp.int32, (8, N), 0)
    lane8 = lax.broadcasted_iota(jnp.int32, (8, N), 1)
    own = BLOCK // 8
    kept_a, kept_m = [], []
    for r0 in range(0, N, BLOCK):
        tall = min(BLOCK + AHEAD, N - r0) // 8
        inside = (lane8 >= r0) & (lane8 < r0 + BLOCK)
        win_s = [work[r0 + 8 * t:r0 + 8 * t + 8, 0:N] for t in range(tall)]
        win_d = [work[r0 + 8 * t:r0 + 8 * t + 8, N:2 * N] for t in range(tall)]
        roots = [root_col[r0 + 8 * t:r0 + 8 * t + 8, :] for t in range(own)]
        cols = [[lane_copy(w, r0 + k) for w in win_s] for k in range(BLOCK)]
        win_s = [jnp.where(inside, jnp.where(lane8 == row8 + (r0 + 8 * t), 1.0, 0.0) if t < own else 0.0, w) for t, w in enumerate(win_s)]
        diag = [jnp.ones((8, N), f32)] * own
        unit = []
        for j in range(0, BLOCK, 2):
            i = j + 1
            home, sj, si = j // 8, j % 8, j % 8 + 1
            cj, ci = cols[j], cols[i]
            a, b, e = row_copy(cj[home], sj), row_copy(cj[home], si), row_copy(ci[home], si)
            det = a * e - b * b
            idet = 1.0 / det
            p, q, r = e * idet, b * idet, a * idet
            ia = 1.0 / a
            ratio = b * ia
            diag[home] = jnp.where(row8 == sj, a, jnp.where(row8 == si, det * ia, diag[home]))
            row_sj, row_si = row_copy(win_s[home], sj), row_copy(win_s[home], si)
            cols_j = {k: row_copy(cols[k][home], sj) for k in range(i + 1, BLOCK)}
            cols_i = {k: row_copy(cols[k][home], si) for k in range(i + 1, BLOCK)}
            unit_j, unit_i = {}, {}
            for t in range(home, tall):
                gj = cj[t] * p - ci[t] * q
                gi = ci[t] * r - cj[t] * q
                gd = cj[t] * ia
                if t == home:
                    below = row8 > si
                    gj, gi = jnp.where(below, gj, 0.0), jnp.where(below, gi, 0.0)
                    gd = jnp.where(row8 > sj, gd, 0.0)
                unit_j[t], unit_i[t] = gd, gi
                if not (t == home and si == 7):
                    for k in range(i + 1, BLOCK):
                        cols[k][t] = cols[k][t] - gj * cols_j[k] - gi * cols_i[k]
                if t == home:
                    gj = jnp.where(row8 == si, ratio, gj)
                win_s[t] = win_s[t] - gj * row_sj - gi * row_si
            unit += [unit_j, unit_i]
        inv = [lax.rsqrt(d) for d in diag]
        f = [d * v for d, v in zip(diag, inv)]
        shrink = [jnp.where(lane8 < M, f[t] / (f[t] + roots[t]), 1.0) for t in range(own)]
        for j in range(BLOCK):
            home = j // 8
            scaled = row_copy(win_d[home] * shrink[home], j % 8)
            for t in unit[j]:
                win_d[t] = win_d[t] - unit[j][t] * scaled
        for t in range(own, tall):
            work[r0 + 8 * t:r0 + 8 * t + 8, 0:N] = win_s[t]
            work[r0 + 8 * t:r0 + 8 * t + 8, N:2 * N] = win_d[t]
        block_s = jnp.concatenate(win_s[:own], axis=0)
        low = r0 + BLOCK + AHEAD
        if low < N:
            left = jnp.concatenate([win_s[t] / diag[t] for t in range(own)], axis=0)
            right = jnp.concatenate([block_s, jnp.concatenate([win_d[t] * shrink[t] for t in range(own)], axis=0)], axis=1)
            update = panel_product(left, right, slice(low, N))
            old = work[low:, 0:N]
            gone = lax.broadcasted_iota(jnp.int32, old.shape, 1)
            work[low:, 0:N] = jnp.where((gone >= r0) & (gone < r0 + BLOCK), 0.0, old) - update[:, 0:N]
            work[low:, N:2 * N] = work[low:, N:2 * N] - update[:, N:2 * N]
        kept_a += [jnp.where(lane8 < r0 + BLOCK, win_s[t] * inv[t], 0.0) for t in range(own)]
        kept_m += [win_d[t] * jnp.where(lane8 < M, -1.0 / (f[t] + roots[t]), inv[t]) for t in range(own)]
        if len(kept_a) == SUMMED // 8:
            a, m = jnp.concatenate(kept_a, axis=0), jnp.concatenate(kept_m, axis=0)
            kept_a, kept_m = [], []
            done = r0 + BLOCK
            update = panel_product(a, jnp.concatenate([a, m], axis=1), slice(0, done))
            if done > SUMMED:
                update = jnp.concatenate([sums[0:done - SUMMED, :] + update[0:done - SUMMED], update[done - SUMMED:]], axis=0)
            sums[0:done, :] = update
        beside(r0 // BLOCK)


def first(b):
    return b * (b + 1) // 2


def rank(x, z, core):
    return (x * Z_DIM + z) * 2 + core


def halves(x):
    h = x.astype(bf16)
    return h, (x - h.astype(f32)).astype(bf16)


def dot3(a, b, cb=0):
    ah, al = halves(a)
    bh, bl = halves(b)
    return dot(jnp.concatenate([ah, al, ah], axis=1), jnp.concatenate([bh, bh, bl], axis=cb), 1, cb, precision=None)


def dot6(a, b, cb=0):
    ah, am, al = (x.astype(bf16) for x in split3(a))
    bh, bm, bl = (x.astype(bf16) for x in split3(b))
    left = jnp.concatenate([ah, ah, am, am, ah, al], axis=1)
    return dot(left, jnp.concatenate([bh, bm, bh, bm, bl, bh], axis=cb), 1, cb, precision=None)


def whole(split):
    lanes = lax.broadcasted_iota(jnp.int32, split.shape, 1)
    return split + jnp.sum(jnp.where(lanes == M, split, 0.0), axis=1, keepdims=True)


def finish(dev, gain, term, cov, weights, old, new, increments):
    cells = old.shape[1]
    held = {}

    def prepare():
        increments(dot6(whole(term()).T[:M], cov(), 1))
        dh, dl = halves(dev()[:, :M])
        held["d"] = jnp.concatenate([dh, dl, dh], axis=1)
        gh, gl = halves(whole(gain()).T[:M] * (1.0 / (M - 1.0)))
        held["g"] = jnp.concatenate([gh, gl, gh], axis=1)
        held["w"] = weights().T
    wide = 4 * N

    def part(index):
        cs = wide * index
        x = old[:, cs:cs + wide]
        xh, xl = halves(x)
        r = dot(held["d"], jnp.concatenate([xh, xh, xl], axis=0), precision=None)
        scale = [jnp.broadcast_to(held["w"][:, t:t + 1], (N, N)) for t in range(cs // N, (cs + wide) // N)]
        rh, rl = halves(r * jnp.concatenate(scale, axis=1))
        new[:, cs:cs + wide] = x + dot(held["g"], jnp.concatenate([rh, rh, rl], axis=0), precision=None)
    return [prepare] + [lambda index=index: part(index) for index in range(cells // wide)]


def kernel(owner_ids, obs_cell, observed, variance, state, weights, post_out, incs, last, last_w, *scratch):
    batches = observed.shape[0]
    tiles = state.shape[1]
    near = scratch[0:batches]
    line = scratch[batches:2 * batches]
    picked = scratch[2 * batches:3 * batches]
    (send, mats, cur, covs, devs, gains, terms, links, sides, work, sums, post, local_w,
        state_sem, weight_sem, push, here) = scratch[3 * batches:]
    h, lev = lax.axis_index("horiz"), lax.axis_index("lev")
    x, z, core = h // (2 * Z_DIM), (h // 2) % Z_DIM, h % 2
    lanes = lax.broadcasted_iota(jnp.int32, (N, N), 1)
    eye = lanes == lax.broadcasted_iota(jnp.int32, (N, N), 0)
    member = lanes < M

    near_peers = [rank((x + s) % X_DIM, z, (core + c) % 2) for s in range(X_DIM) for c in range(2) if s or c]
    near_peers = [{"horiz": to, "lev": lev} for to in near_peers]
    line_peers = [{"horiz": rank(x, (z + s) % Z_DIM, core), "lev": lev} for s in range(1, Z_DIM)]
    level_peers = [{"horiz": h, "lev": (lev + s) % Y_DIM} for s in range(1, Y_DIM)]
    peers = [near_peers, line_peers, level_peers, [{"horiz": rank(x, z, 1 - core), "lev": lev}]]

    barrier = pltpu.get_barrier_semaphore()
    for to in near_peers + line_peers + level_peers:
        pl.semaphore_signal(barrier, inc=1, device_id=to, device_id_type=MESH)

    def slab(t):
        return pltpu.make_async_copy(state.at[:, t, :], post.at[:, t * N:(t + 1) * N], state_sem.at[t])
    def onward(k):
        chunk = slice(4 * N * k, 4 * N * (k + 1))
        return pltpu.make_async_copy(post.at[:, chunk], post_out.at[:, chunk], state_sem.at[k])
    fetch = pltpu.make_async_copy(weights, local_w, weight_sem)

    def shared(b):
        return b >= WHOLE_GROUPS

    def half(b, which):
        rows = PER_LEVEL // 2
        return pl.ds(pl.multiple_of(which * rows, rows), rows) if shared(b) else slice(None)

    def group(b):
        return slice(first(b), first(b + 1))

    def copies(b, stage):
        if stage == 0:
            source, target = send.at[group(b)], near[b].at[x * 2 + core]
        elif stage == 1:
            source, target = picked[b].at[:, half(b, core)], line[b].at[z]
        elif stage == 2:
            source, target = line[b].at[Z_DIM], mats.at[group(b), lev, half(b, core)]
        else:
            source = target = mats.at[group(b), :, half(b, core)]
        return [
            pltpu.make_async_remote_copy(source, target, push.at[b, stage, i], here.at[b, stage], device_id=to, device_id_type=MESH)
            for i, to in enumerate(peers[stage])
        ]

    def start(b, stage):
        owner = owner_ids[b]
        if stage == 0:
            near[b][x * 2 + core] = send[group(b)]
        elif stage == 1:
            picked[b][...] = near[b][(owner // (2 * Z_DIM)) * 2 + owner % 2]
            line[b][z] = picked[b][:, half(b, core)]
        elif stage == 2:
            block = line[b][(owner // 2) % Z_DIM]
            line[b][Z_DIM] = block
            mats[group(b), lev, half(b, core)] = block
        for copy in copies(b, stage):
            copy.start()

    def arrived(b, stage):
        count = len(peers[stage])
        if stage < 2:
            whole = [near, line][stage][b].at[0:count]
        else:
            whole = mats.at[group(b), 0:count, half(b, core)] if stage == 2 else mats.at[group(b), :, half(b, 1 - core)]
        pltpu.make_async_copy(whole, whole, here.at[b, stage]).wait()

    def advance(b, stage):
        if b < batches:
            if stage > 0:
                arrived(b, stage - 1)
            start(b, stage)

    def arrive(c):
        arrived(c, 3 if shared(c) else 2)
        cur[c] = centred(mats[first(c)].reshape(N, N))

    def weight(c, a):
        return mats[first(c) + 1 + a].reshape(N, N)

    def column(row):
        return jnp.sum(jnp.where(eye, row, 0.0), axis=1, keepdims=True)

    def take_sides(b):
        var_col = column(variance[b:b + 1, :])
        sides[b, 0] = jnp.broadcast_to(var_col, (N, N))
        sides[b, 1] = jnp.broadcast_to(jnp.sqrt(var_col), (N, N))
        sides[b, 2] = jnp.broadcast_to(column(observed[b:b + 1, :]), (N, N))

    def centred(priors):
        mean = jnp.sum(jnp.where(member, priors, 0.0), axis=1, keepdims=True) / M
        return jnp.where(member, priors - mean, jnp.where(lanes == M, mean, 0.0))

    def link(c, a):
        return dot3(cur[c], devs[a], 1) * weight(c, a) * (1.0 / (M - 1.0))

    def carry_over(c, a):
        cur[c] = cur[c] + dot3(link(c, a), gains[a])

    def batch(b, services):
        blocks = N // BLOCK
        share = [[] for _ in range(blocks + 2)]
        if b > 0:
            def keep(value):
                incs[b - 1] = value
            before = finish(*[lambda ref=ref: ref[b - 1] for ref in (devs, gains, terms, covs, local_w)], post, post, keep)
            for k, step in enumerate(before):
                if b == batches - 1 and k > 0:
                    step = lambda k=k, step=step: (step(), onward(k - 1).start())
                share[PLACES[k]].append(step)
        if b + 1 < batches:
            at = ARRIVAL[b]
            share[at].append(lambda: arrive(b + 1))
            for a in range(b):
                share[min(at + a, blocks - 1)].append(lambda a=a: carry_over(b + 1, a))

            def last_link():
                links[b] = link(b + 1, b)
            share[min(at + b, blocks - 1)].append(last_link)

        def beside(block):
            for group_moved, stage in services.get(block, ()):
                advance(group_moved, stage)
            for step in share[block]:
                step()
        p = cur[b]
        devs[b] = jnp.where(member, p, 0.0)
        dev = devs[b]
        var_row = variance[b:b + 1, :]
        cov = dot6(dev, dev, 1) * (1.0 / (M - 1.0))
        covs[b] = cov
        work[:, 0:N] = jnp.where(eye, cov + var_row, cov)
        work[:, N:2 * N] = jnp.where(lanes == M, sides[b, 2] - p, dev)
        eliminate(work, sums, sides.at[b, 1], beside)
        t = sums[:, N:2 * N]
        terms[b] = t
        beside(blocks)
        gain = t - dot6(sums[:, 0:N], sides[b, 0] * t)
        gains[b] = gain
        beside(blocks + 1)
        if b + 1 < batches:
            cur[b + 1] = cur[b + 1] + dot3(links[b], gain)

    for t in range(tiles):
        slab(t).start()
    fetch.start()
    row_lanes = lax.broadcasted_iota(jnp.int32, (8, N), 1)
    cells = jnp.zeros((8, N), jnp.int32)
    for b in range(batches):
        turned = pltpu.roll(jnp.broadcast_to(obs_cell[b:b + 1, :], (8, N)), (b * PER_LEVEL - lev * PER_LEVEL + N) % N, 1)
        cells = jnp.where((row_lanes >= b * PER_LEVEL) & (row_lanes < (b + 1) * PER_LEVEL), turned, cells)
    cells = cells[0:1]
    tile_of = column((cells // TILE).astype(f32))
    in_tile = jnp.where(lax.broadcasted_iota(jnp.int32, (N, tiles), 1).astype(f32) == tile_of, 1.0, 0.0)
    wide = 4 * N
    gathered = jnp.zeros((3 * M, N), f32)
    for cs in range(0, tiles * N, wide):
        for t in range(cs // N, (cs + wide) // N):
            slab(t).wait()
        parts = jnp.concatenate(split3(post[:, cs:cs + wide]), axis=0).astype(bf16)
        chosen = jnp.where(lax.broadcasted_iota(jnp.int32, (wide, N), 0) + cs == cells, 1.0, 0.0).astype(bf16)
        gathered = gathered + dot(parts, chosen, precision=None)
    gathered = gathered[:M] + gathered[M:2 * M] + gathered[2 * M:]
    rows = jnp.concatenate([gathered, jnp.zeros((N - M, N), f32)], axis=0).T
    for b in range(batches):
        send[first(b)] = rows[b * PER_LEVEL:(b + 1) * PER_LEVEL]
    pl.semaphore_wait(barrier, len(near_peers) + len(line_peers) + len(level_peers))
    advance(0, 0)
    fetch.wait()
    for a in range(batches - 1):
        rows = dot(in_tile, local_w[a])
        for b in range(a + 1, batches):
            send[first(b) + 1 + a] = rows[b * PER_LEVEL:(b + 1) * PER_LEVEL]
    advance(1, 0)
    advance(2, 0)
    for b in range(batches):
        take_sides(b)
    advance(0, 1)
    advance(1, 1)
    advance(3, 0)
    advance(0, 2)
    advance(2, 1)
    advance(1, 2)
    advance(4, 0)
    arrive(0)
    services = SERVICES
    for b in range(batches):
        batch(b, services.get(b, {}))
    for k, ref in enumerate((devs, gains, terms, covs)):
        last[k] = ref[batches - 1]
    last_w[...] = local_w[batches - 1]
    for k in range(tiles // 4):
        onward(k).wait()
    for b in range(batches):
        for stage in range(4 if shared(b) else 3):
            for copy in copies(b, stage):
                copy.wait_send()


def last_kernel(slab, incs, factors, weights, state_out, incs_out, old, new, held, held_w, held_incs, state_sem, slab_sem, small_sem):
    batches = incs.shape[0]
    tiles = state_out.shape[1]

    def inward(k):
        chunk = slice(4 * N * k, 4 * N * (k + 1))
        return pltpu.make_async_copy(slab.at[:, chunk], old.at[:, chunk], slab_sem.at[k])

    def outward(t):
        return pltpu.make_async_copy(new.at[:, t * N:(t + 1) * N], state_out.at[:, t, :], state_sem.at[t])
    small = [
        pltpu.make_async_copy(factors, held, small_sem.at[0]),
        pltpu.make_async_copy(weights, held_w, small_sem.at[1]),
        pltpu.make_async_copy(incs.at[0:batches - 1], held_incs.at[0:batches - 1], small_sem.at[2]),
    ]
    away = pltpu.make_async_copy(held_incs, incs_out, small_sem.at[3])
    for copy in small[:2] + [inward(k) for k in range(tiles // 4)] + small[2:]:
        copy.start()

    def keep(value):
        held_incs[batches - 1] = value
    steps = finish(*[lambda k=k: held[k] for k in range(4)], lambda: held_w[...], old, new, keep)
    for copy in small[:2]:
        copy.wait()
    for k, step in enumerate(steps):
        if k == 0:
            step()
            small[2].wait()
            away.start()
            for part in range(tiles // 4):
                inward(part).wait()
        else:
            step()
        if k > 0 and k % GROUPED == 0:
            for t in range(4 * (k - GROUPED), 4 * k):
                outward(t).start()
    away.wait()
    for t in range(tiles):
        outward(t).wait()


def conclude(slab, incs, factors, weights, state_shape):
    hbm = pl.BlockSpec(memory_space=pltpu.MemorySpace.HBM)
    dma = pltpu.SemaphoreType.DMA
    return pl.pallas_call(
        last_kernel,
        out_shape=(jax.ShapeDtypeStruct(state_shape, f32), jax.ShapeDtypeStruct(incs.shape, f32)),
        in_specs=[hbm] * 4,
        out_specs=(hbm, hbm),
        scratch_shapes=[pltpu.VMEM(ref.shape, f32) for ref in (slab, slab, factors, weights)] + [
            pltpu.VMEM(incs.shape, f32), dma((state_shape[1],)), dma((state_shape[1] // 4,)), dma((4,)),
        ],
        compiler_params=pltpu.CompilerParams(vmem_limit_bytes=60 << 20),
    )(slab, incs, factors, weights)


def assimilate(owner_ids, obs_cell, observed, variance, state, weights):
    batches = observed.shape[0]
    tiles = state.shape[1]
    vm = pl.BlockSpec(memory_space=pltpu.VMEM)
    smem = pl.BlockSpec(memory_space=pltpu.SMEM)
    hbm = pl.BlockSpec(memory_space=pltpu.MemorySpace.HBM)
    dma = pltpu.SemaphoreType.DMA

    def block(*lead):
        return pltpu.VMEM((*lead, N), f32)
    groups = [(b + 1, PER_LEVEL) for b in range(batches)]
    parts = [(b + 1, PER_LEVEL // (1 if b < WHOLE_GROUPS else 2)) for b in range(batches)]
    return pl.pallas_call(
        kernel,
        out_shape=tuple(jax.ShapeDtypeStruct(shape, f32) for shape in (
            (M, tiles * N), (batches, M, N), (4, N, N), (tiles, N))),
        in_specs=[smem, vm, vm, vm, hbm, hbm],
        out_specs=(hbm, vm, vm, vm),
        scratch_shapes=[block(2 * X_DIM, *g) for g in groups] + [block(Z_DIM + 1, *g) for g in parts] + [block(*g) for g in groups] + [
            block(first(batches), PER_LEVEL), block(first(batches), Y_DIM, PER_LEVEL)] + [block(batches, N)] * 6 + [block(batches, 3, N)] + [
            pltpu.VMEM((N, 2 * N), f32), pltpu.VMEM((N, 2 * N), f32), pltpu.VMEM((M, tiles * N), f32), block(batches, tiles),
            dma((tiles,)), dma, dma((batches, 4, max(2 * X_DIM, Z_DIM, Y_DIM) - 1)), dma((batches, 4)),
        ],
        compiler_params=pltpu.CompilerParams(vmem_limit_bytes=60 << 20, collective_id=0, has_side_effects=True),
        cost_estimate=pl.CostEstimate(flops=10**9, bytes_accessed=4 * 10**6, transcendentals=0),
    )(owner_ids, obs_cell, observed, variance, state, weights)


def local(prior_state, localization, observed, error_variance, owner_ids, obs_cell):
    members, _, cells = prior_state.shape
    tiles = cells // TILE
    batches = obs_cell.shape[0]
    weights = jnp.transpose(localization.reshape(batches, N, tiles), (0, 2, 1))
    state = prior_state.reshape(members, tiles, TILE)
    slab, increments, factors, last_weights = assimilate(owner_ids, obs_cell, observed, error_variance, state, weights)
    state, increments = conclude(slab, increments, factors, last_weights, state.shape)
    return state.reshape(members, 1, cells), jnp.transpose(increments, (0, 2, 1))


def solution(mesh):
    in_specs = (P(None, "lev", "horiz"), P(None, None, "lev", "horiz"), P(), P(), P(), P())
    out_specs = (P(None, "lev", "horiz"), P())
    return jax.shard_map(local, mesh=mesh, in_specs=in_specs, out_specs=out_specs, check_vma=False)
```

```python
import jax
import jax.numpy as jnp
from jax import lax
from jax.experimental import pallas as pl
from jax.experimental.pallas import tpu as pltpu
from jax.sharding import PartitionSpec as P

f32 = jnp.float32
bf16 = jnp.bfloat16
HI = lax.Precision.HIGHEST
MESH = pl.DeviceIdType.MESH
X_DIM, Z_DIM, Y_DIM = 4, 8, 8
TILE = 128
N, M = 128, 80
PER_LEVEL = N // Y_DIM
WHOLE_GROUPS = 2
GROUPED = 4
PLACES = (0, 0, 1, 2, 3, 4, 6, 8, 9)
ARRIVAL = (7, 5, 3, 6, 4)
SERVICES = {
    0: {2: [(4, 1), (5, 0)], 5: [(3, 2)], 6: [(5, 1)]},
    1: {2: [(2, 3)], 7: [(4, 2)]},
    2: {1: [(3, 3)], 4: [(5, 2)]},
    3: {4: [(4, 3)]},
    4: {2: [(5, 3)]},
}


def dot(a, b, ca=1, cb=0, precision=HI):
    return lax.dot_general(a, b, (((ca,), (cb,)), ((), ())), precision=precision, preferred_element_type=f32)


def split3(x):
    h = x.astype(bf16).astype(f32)
    r = x - h
    m = r.astype(bf16).astype(f32)
    return h, m, r - m


def panel_product(left, right, rows):
    h, m, l = split3(left)
    lhs = jnp.concatenate([h, h, m, m, h, l], axis=0).T[rows].astype(bf16)
    h, m, l = split3(right)
    rhs = jnp.concatenate([h, m, h, m, l, h], axis=0).astype(bf16)
    return lax.dot_general(lhs, rhs, (((1,), (0,)), ((), ())), preferred_element_type=f32)


BLOCK = 16
AHEAD = 16
SUMMED = 16


def lane_copy(tile, lane):
    return jnp.take_along_axis(tile, jnp.full(tile.shape, lane, jnp.int32), axis=1)


def row_copy(tile, row):
    return jnp.broadcast_to(tile[row:row + 1], tile.shape)


def eliminate(work, sums, root_col, beside):
    row8 = lax.broadcasted_iota(jnp.int32, (8, N), 0)
    lane8 = lax.broadcasted_iota(jnp.int32, (8, N), 1)
    own = BLOCK // 8
    kept_a, kept_m = [], []
    for r0 in range(0, N, BLOCK):
        tall = min(BLOCK + AHEAD, N - r0) // 8
        inside = (lane8 >= r0) & (lane8 < r0 + BLOCK)
        win_s = [work[r0 + 8 * t:r0 + 8 * t + 8, 0:N] for t in range(tall)]
        win_d = [work[r0 + 8 * t:r0 + 8 * t + 8, N:2 * N] for t in range(tall)]
        roots = [root_col[r0 + 8 * t:r0 + 8 * t + 8, :] for t in range(own)]
        cols = [[lane_copy(w, r0 + k) for w in win_s] for k in range(BLOCK)]
        win_s = [jnp.where(inside, jnp.where(lane8 == row8 + (r0 + 8 * t), 1.0, 0.0) if t < own else 0.0, w) for t, w in enumerate(win_s)]
        diag = [jnp.ones((8, N), f32)] * own
        unit = []
        for j in range(0, BLOCK, 2):
            i = j + 1
            home, sj, si = j // 8, j % 8, j % 8 + 1
            cj, ci = cols[j], cols[i]
            a, b, e = row_copy(cj[home], sj), row_copy(cj[home], si), row_copy(ci[home], si)
            det = a * e - b * b
            idet = 1.0 / det
            p, q, r = e * idet, b * idet, a * idet
            ia = 1.0 / a
            ratio = b * ia
            diag[home] = jnp.where(row8 == sj, a, jnp.where(row8 == si, det * ia, diag[home]))
            row_sj, row_si = row_copy(win_s[home], sj), row_copy(win_s[home], si)
            cols_j = {k: row_copy(cols[k][home], sj) for k in range(i + 1, BLOCK)}
            cols_i = {k: row_copy(cols[k][home], si) for k in range(i + 1, BLOCK)}
            unit_j, unit_i = {}, {}
            for t in range(home, tall):
                gj = cj[t] * p - ci[t] * q
                gi = ci[t] * r - cj[t] * q
                gd = cj[t] * ia
                if t == home:
                    below = row8 > si
                    gj, gi = jnp.where(below, gj, 0.0), jnp.where(below, gi, 0.0)
                    gd = jnp.where(row8 > sj, gd, 0.0)
                unit_j[t], unit_i[t] = gd, gi
                if not (t == home and si == 7):
                    for k in range(i + 1, BLOCK):
                        cols[k][t] = cols[k][t] - gj * cols_j[k] - gi * cols_i[k]
                if t == home:
                    gj = jnp.where(row8 == si, ratio, gj)
                win_s[t] = win_s[t] - gj * row_sj - gi * row_si
            unit += [unit_j, unit_i]
        inv = [lax.rsqrt(d) for d in diag]
        f = [d * v for d, v in zip(diag, inv)]
        shrink = [jnp.where(lane8 < M, f[t] / (f[t] + roots[t]), 1.0) for t in range(own)]
        for j in range(BLOCK):
            home = j // 8
            scaled = row_copy(win_d[home] * shrink[home], j % 8)
            for t in unit[j]:
                win_d[t] = win_d[t] - unit[j][t] * scaled
        for t in range(own, tall):
            work[r0 + 8 * t:r0 + 8 * t + 8, 0:N] = win_s[t]
            work[r0 + 8 * t:r0 + 8 * t + 8, N:2 * N] = win_d[t]
        block_s = jnp.concatenate(win_s[:own], axis=0)
        low = r0 + BLOCK + AHEAD
        if low < N:
            left = jnp.concatenate([win_s[t] / diag[t] for t in range(own)], axis=0)
            right = jnp.concatenate([block_s, jnp.concatenate([win_d[t] * shrink[t] for t in range(own)], axis=0)], axis=1)
            update = panel_product(left, right, slice(low, N))
            old = work[low:, 0:N]
            gone = lax.broadcasted_iota(jnp.int32, old.shape, 1)
            work[low:, 0:N] = jnp.where((gone >= r0) & (gone < r0 + BLOCK), 0.0, old) - update[:, 0:N]
            work[low:, N:2 * N] = work[low:, N:2 * N] - update[:, N:2 * N]
        kept_a += [jnp.where(lane8 < r0 + BLOCK, win_s[t] * inv[t], 0.0) for t in range(own)]
        kept_m += [win_d[t] * jnp.where(lane8 < M, -1.0 / (f[t] + roots[t]), inv[t]) for t in range(own)]
        if len(kept_a) == SUMMED // 8:
            a, m = jnp.concatenate(kept_a, axis=0), jnp.concatenate(kept_m, axis=0)
            kept_a, kept_m = [], []
            done = r0 + BLOCK
            update = panel_product(a, jnp.concatenate([a, m], axis=1), slice(0, done))
            if done > SUMMED:
                update = jnp.concatenate([sums[0:done - SUMMED, :] + update[0:done - SUMMED], update[done - SUMMED:]], axis=0)
            sums[0:done, :] = update
        beside(r0 // BLOCK)


def first(b):
    return b * (b + 1) // 2


def rank(x, z, core):
    return (x * Z_DIM + z) * 2 + core


def halves(x):
    h = x.astype(bf16)
    return h, (x - h.astype(f32)).astype(bf16)


def dot3(a, b, cb=0):
    ah, al = halves(a)
    bh, bl = halves(b)
    return dot(jnp.concatenate([ah, al, ah], axis=1), jnp.concatenate([bh, bh, bl], axis=cb), 1, cb, precision=None)


def dot6(a, b, cb=0):
    ah, am, al = (x.astype(bf16) for x in split3(a))
    bh, bm, bl = (x.astype(bf16) for x in split3(b))
    left = jnp.concatenate([ah, ah, am, am, ah, al], axis=1)
    return dot(left, jnp.concatenate([bh, bm, bh, bm, bl, bh], axis=cb), 1, cb, precision=None)


def whole(split):
    lanes = lax.broadcasted_iota(jnp.int32, split.shape, 1)
    return split + jnp.sum(jnp.where(lanes == M, split, 0.0), axis=1, keepdims=True)


def finish(dev, gain, term, cov, weights, old, new, increments):
    cells = old.shape[1]
    held = {}

    def prepare():
        increments(dot6(whole(term()).T[:M], cov(), 1))
        dh, dl = halves(dev()[:, :M])
        held["d"] = jnp.concatenate([dh, dl, dh], axis=1)
        gh, gl = halves(whole(gain()).T[:M] * (1.0 / (M - 1.0)))
        held["g"] = jnp.concatenate([gh, gl, gh], axis=1)
        held["w"] = weights().T
    wide = 4 * N

    def part(index):
        cs = wide * index
        x = old[:, cs:cs + wide]
        xh, xl = halves(x)
        r = dot(held["d"], jnp.concatenate([xh, xh, xl], axis=0), precision=None)
        scale = [jnp.broadcast_to(held["w"][:, t:t + 1], (N, N)) for t in range(cs // N, (cs + wide) // N)]
        rh, rl = halves(r * jnp.concatenate(scale, axis=1))
        new[:, cs:cs + wide] = x + dot(held["g"], jnp.concatenate([rh, rh, rl], axis=0), precision=None)
    return [prepare] + [lambda index=index: part(index) for index in range(cells // wide)]


def kernel(owner_ids, obs_cell, observed, variance, state, weights, post_out, incs, last, last_w, *scratch):
    batches = observed.shape[0]
    tiles = state.shape[1]
    near = scratch[0:batches]
    line = scratch[batches:2 * batches]
    picked = scratch[2 * batches:3 * batches]
    (send, mats, cur, covs, devs, gains, terms, links, sides, work, sums, post, local_w,
        state_sem, weight_sem, push, here) = scratch[3 * batches:]
    h, lev = lax.axis_index("horiz"), lax.axis_index("lev")
    x, z, core = h // (2 * Z_DIM), (h // 2) % Z_DIM, h % 2
    lanes = lax.broadcasted_iota(jnp.int32, (N, N), 1)
    eye = lanes == lax.broadcasted_iota(jnp.int32, (N, N), 0)
    member = lanes < M

    near_peers = [rank((x + s) % X_DIM, z, (core + c) % 2) for s in range(X_DIM) for c in range(2) if s or c]
    near_peers = [{"horiz": to, "lev": lev} for to in near_peers]
    line_peers = [{"horiz": rank(x, (z + s) % Z_DIM, core), "lev": lev} for s in range(1, Z_DIM)]
    level_peers = [{"horiz": h, "lev": (lev + s) % Y_DIM} for s in range(1, Y_DIM)]
    peers = [near_peers, line_peers, level_peers, [{"horiz": rank(x, z, 1 - core), "lev": lev}]]

    barrier = pltpu.get_barrier_semaphore()
    for to in near_peers + line_peers + level_peers:
        pl.semaphore_signal(barrier, inc=1, device_id=to, device_id_type=MESH)

    def slab(t):
        return pltpu.make_async_copy(state.at[:, t, :], post.at[:, t * N:(t + 1) * N], state_sem.at[t])
    def onward(k):
        chunk = slice(4 * N * k, 4 * N * (k + 1))
        return pltpu.make_async_copy(post.at[:, chunk], post_out.at[:, chunk], state_sem.at[k])
    fetch = pltpu.make_async_copy(weights, local_w, weight_sem)

    def shared(b):
        return b >= WHOLE_GROUPS

    def half(b, which):
        rows = PER_LEVEL // 2
        return pl.ds(pl.multiple_of(which * rows, rows), rows) if shared(b) else slice(None)

    def group(b):
        return slice(first(b), first(b + 1))

    def copies(b, stage):
        if stage == 0:
            source, target = send.at[group(b)], near[b].at[x * 2 + core]
        elif stage == 1:
            source, target = picked[b].at[:, half(b, core)], line[b].at[z]
        elif stage == 2:
            source, target = line[b].at[Z_DIM], mats.at[group(b), lev, half(b, core)]
        else:
            source = target = mats.at[group(b), :, half(b, core)]
        return [
            pltpu.make_async_remote_copy(source, target, push.at[b, stage, i], here.at[b, stage], device_id=to, device_id_type=MESH)
            for i, to in enumerate(peers[stage])
        ]

    def start(b, stage):
        owner = owner_ids[b]
        if stage == 0:
            near[b][x * 2 + core] = send[group(b)]
        elif stage == 1:
            picked[b][...] = near[b][(owner // (2 * Z_DIM)) * 2 + owner % 2]
            line[b][z] = picked[b][:, half(b, core)]
        elif stage == 2:
            block = line[b][(owner // 2) % Z_DIM]
            line[b][Z_DIM] = block
            mats[group(b), lev, half(b, core)] = block
        for copy in copies(b, stage):
            copy.start()

    def arrived(b, stage):
        count = len(peers[stage])
        if stage < 2:
            whole = [near, line][stage][b].at[0:count]
        else:
            whole = mats.at[group(b), 0:count, half(b, core)] if stage == 2 else mats.at[group(b), :, half(b, 1 - core)]
        pltpu.make_async_copy(whole, whole, here.at[b, stage]).wait()

    def advance(b, stage):
        if b < batches:
            if stage > 0:
                arrived(b, stage - 1)
            start(b, stage)

    def arrive(c):
        arrived(c, 3 if shared(c) else 2)
        cur[c] = centred(mats[first(c)].reshape(N, N))

    def weight(c, a):
        return mats[first(c) + 1 + a].reshape(N, N)

    def column(row):
        return jnp.sum(jnp.where(eye, row, 0.0), axis=1, keepdims=True)

    def take_sides(b):
        var_col = column(variance[b:b + 1, :])
        sides[b, 0] = jnp.broadcast_to(var_col, (N, N))
        sides[b, 1] = jnp.broadcast_to(jnp.sqrt(var_col), (N, N))
        sides[b, 2] = jnp.broadcast_to(column(observed[b:b + 1, :]), (N, N))

    def centred(priors):
        mean = jnp.sum(jnp.where(member, priors, 0.0), axis=1, keepdims=True) / M
        return jnp.where(member, priors - mean, jnp.where(lanes == M, mean, 0.0))

    def link(c, a):
        return dot3(cur[c], devs[a], 1) * weight(c, a) * (1.0 / (M - 1.0))

    def carry_over(c, a):
        cur[c] = cur[c] + dot3(link(c, a), gains[a])

    def batch(b, services):
        blocks = N // BLOCK
        share = [[] for _ in range(blocks + 2)]
        if b > 0:
            def keep(value):
                incs[b - 1] = value
            before = finish(*[lambda ref=ref: ref[b - 1] for ref in (devs, gains, terms, covs, local_w)], post, post, keep)
            for k, step in enumerate(before):
                if b == batches - 1 and k > 0:
                    step = lambda k=k, step=step: (step(), onward(k - 1).start())
                share[PLACES[k]].append(step)
        if b + 1 < batches:
            at = ARRIVAL[b]
            share[at].append(lambda: arrive(b + 1))
            for a in range(b):
                share[min(at + a, blocks - 1)].append(lambda a=a: carry_over(b + 1, a))

            def last_link():
                links[b] = link(b + 1, b)
            share[min(at + b, blocks - 1)].append(last_link)

        def beside(block):
            for group_moved, stage in services.get(block, ()):
                advance(group_moved, stage)
            for step in share[block]:
                step()
        p = cur[b]
        devs[b] = jnp.where(member, p, 0.0)
        dev = devs[b]
        var_row = variance[b:b + 1, :]
        cov = dot6(dev, dev, 1) * (1.0 / (M - 1.0))
        covs[b] = cov
        work[:, 0:N] = jnp.where(eye, cov + var_row, cov)
        work[:, N:2 * N] = jnp.where(lanes == M, sides[b, 2] - p, dev)
        eliminate(work, sums, sides.at[b, 1], beside)
        t = sums[:, N:2 * N]
        terms[b] = t
        beside(blocks)
        gain = t - dot6(sums[:, 0:N], sides[b, 0] * t)
        gains[b] = gain
        beside(blocks + 1)
        if b + 1 < batches:
            cur[b + 1] = cur[b + 1] + dot3(links[b], gain)

    for t in range(tiles):
        slab(t).start()
    fetch.start()
    row_lanes = lax.broadcasted_iota(jnp.int32, (8, N), 1)
    cells = jnp.zeros((8, N), jnp.int32)
    for b in range(batches):
        turned = pltpu.roll(jnp.broadcast_to(obs_cell[b:b + 1, :], (8, N)), (b * PER_LEVEL - lev * PER_LEVEL + N) % N, 1)
        cells = jnp.where((row_lanes >= b * PER_LEVEL) & (row_lanes < (b + 1) * PER_LEVEL), turned, cells)
    cells = cells[0:1]
    tile_of = column((cells // TILE).astype(f32))
    in_tile = jnp.where(lax.broadcasted_iota(jnp.int32, (N, tiles), 1).astype(f32) == tile_of, 1.0, 0.0)
    wide = 4 * N
    gathered = jnp.zeros((3 * M, N), f32)
    for cs in range(0, tiles * N, wide):
        for t in range(cs // N, (cs + wide) // N):
            slab(t).wait()
        parts = jnp.concatenate(split3(post[:, cs:cs + wide]), axis=0).astype(bf16)
        chosen = jnp.where(lax.broadcasted_iota(jnp.int32, (wide, N), 0) + cs == cells, 1.0, 0.0).astype(bf16)
        gathered = gathered + dot(parts, chosen, precision=None)
    gathered = gathered[:M] + gathered[M:2 * M] + gathered[2 * M:]
    rows = jnp.concatenate([gathered, jnp.zeros((N - M, N), f32)], axis=0).T
    for b in range(batches):
        send[first(b)] = rows[b * PER_LEVEL:(b + 1) * PER_LEVEL]
    pl.semaphore_wait(barrier, len(near_peers) + len(line_peers) + len(level_peers))
    advance(0, 0)
    fetch.wait()
    for a in range(batches - 1):
        rows = dot(in_tile, local_w[a])
        for b in range(a + 1, batches):
            send[first(b) + 1 + a] = rows[b * PER_LEVEL:(b + 1) * PER_LEVEL]
    advance(1, 0)
    advance(2, 0)
    for b in range(batches):
        take_sides(b)
    advance(0, 1)
    advance(1, 1)
    advance(3, 0)
    advance(2, 1)
    advance(0, 2)
    advance(4, 0)
    advance(1, 2)
    advance(3, 1)
    advance(2, 2)
    arrive(0)
    services = SERVICES
    for b in range(batches):
        batch(b, services.get(b, {}))
    for k, ref in enumerate((devs, gains, terms, covs)):
        last[k] = ref[batches - 1]
    last_w[...] = local_w[batches - 1]
    for k in range(tiles // 4):
        onward(k).wait()
    for b in range(batches):
        for stage in range(4 if shared(b) else 3):
            for copy in copies(b, stage):
                copy.wait_send()


def last_kernel(slab, incs, factors, weights, state_out, incs_out, old, new, held, held_w, held_incs, state_sem, slab_sem, small_sem):
    batches = incs.shape[0]
    tiles = state_out.shape[1]

    def inward(k):
        chunk = slice(4 * N * k, 4 * N * (k + 1))
        return pltpu.make_async_copy(slab.at[:, chunk], old.at[:, chunk], slab_sem.at[k])

    def outward(t):
        return pltpu.make_async_copy(new.at[:, t * N:(t + 1) * N], state_out.at[:, t, :], state_sem.at[t])
    small = [
        pltpu.make_async_copy(factors, held, small_sem.at[0]),
        pltpu.make_async_copy(weights, held_w, small_sem.at[1]),
        pltpu.make_async_copy(incs.at[0:batches - 1], held_incs.at[0:batches - 1], small_sem.at[2]),
    ]
    away = pltpu.make_async_copy(held_incs, incs_out, small_sem.at[3])
    for copy in small[:2] + [inward(k) for k in range(tiles // 4)] + small[2:]:
        copy.start()

    def keep(value):
        held_incs[batches - 1] = value
    steps = finish(*[lambda k=k: held[k] for k in range(4)], lambda: held_w[...], old, new, keep)
    for copy in small[:2]:
        copy.wait()
    for k, step in enumerate(steps):
        if k == 0:
            step()
            small[2].wait()
            away.start()
            for part in range(tiles // 4):
                inward(part).wait()
        else:
            step()
        if k > 0 and k % GROUPED == 0:
            for t in range(4 * (k - GROUPED), 4 * k):
                outward(t).start()
    away.wait()
    for t in range(tiles):
        outward(t).wait()


def conclude(slab, incs, factors, weights, state_shape):
    hbm = pl.BlockSpec(memory_space=pltpu.MemorySpace.HBM)
    dma = pltpu.SemaphoreType.DMA
    return pl.pallas_call(
        last_kernel,
        out_shape=(jax.ShapeDtypeStruct(state_shape, f32), jax.ShapeDtypeStruct(incs.shape, f32)),
        in_specs=[hbm] * 4,
        out_specs=(hbm, hbm),
        scratch_shapes=[pltpu.VMEM(ref.shape, f32) for ref in (slab, slab, factors, weights)] + [
            pltpu.VMEM(incs.shape, f32), dma((state_shape[1],)), dma((state_shape[1] // 4,)), dma((4,)),
        ],
        compiler_params=pltpu.CompilerParams(vmem_limit_bytes=60 << 20),
    )(slab, incs, factors, weights)


def assimilate(owner_ids, obs_cell, observed, variance, state, weights):
    batches = observed.shape[0]
    tiles = state.shape[1]
    vm = pl.BlockSpec(memory_space=pltpu.VMEM)
    smem = pl.BlockSpec(memory_space=pltpu.SMEM)
    hbm = pl.BlockSpec(memory_space=pltpu.MemorySpace.HBM)
    dma = pltpu.SemaphoreType.DMA

    def block(*lead):
        return pltpu.VMEM((*lead, N), f32)
    groups = [(b + 1, PER_LEVEL) for b in range(batches)]
    parts = [(b + 1, PER_LEVEL // (1 if b < WHOLE_GROUPS else 2)) for b in range(batches)]
    return pl.pallas_call(
        kernel,
        out_shape=tuple(jax.ShapeDtypeStruct(shape, f32) for shape in (
            (M, tiles * N), (batches, M, N), (4, N, N), (tiles, N))),
        in_specs=[smem, vm, vm, vm, hbm, hbm],
        out_specs=(hbm, vm, vm, vm),
        scratch_shapes=[block(2 * X_DIM, *g) for g in groups] + [block(Z_DIM + 1, *g) for g in parts] + [block(*g) for g in groups] + [
            block(first(batches), PER_LEVEL), block(first(batches), Y_DIM, PER_LEVEL)] + [block(batches, N)] * 6 + [block(batches, 3, N)] + [
            pltpu.VMEM((N, 2 * N), f32), pltpu.VMEM((N, 2 * N), f32), pltpu.VMEM((M, tiles * N), f32), block(batches, tiles),
            dma((tiles,)), dma, dma((batches, 4, max(2 * X_DIM, Z_DIM, Y_DIM) - 1)), dma((batches, 4)),
        ],
        compiler_params=pltpu.CompilerParams(vmem_limit_bytes=60 << 20, collective_id=0, has_side_effects=True),
        cost_estimate=pl.CostEstimate(flops=10**9, bytes_accessed=4 * 10**6, transcendentals=0),
    )(owner_ids, obs_cell, observed, variance, state, weights)


def local(prior_state, localization, observed, error_variance, owner_ids, obs_cell):
    members, _, cells = prior_state.shape
    tiles = cells // TILE
    batches = obs_cell.shape[0]
    weights = jnp.transpose(localization.reshape(batches, N, tiles), (0, 2, 1))
    state = prior_state.reshape(members, tiles, TILE)
    slab, increments, factors, last_weights = assimilate(owner_ids, obs_cell, observed, error_variance, state, weights)
    state, increments = conclude(slab, increments, factors, last_weights, state.shape)
    return state.reshape(members, 1, cells), jnp.transpose(increments, (0, 2, 1))


def solution(mesh):
    in_specs = (P(None, "lev", "horiz"), P(None, None, "lev", "horiz"), P(), P(), P(), P())
    out_specs = (P(None, "lev", "horiz"), P())
    return jax.shard_map(local, mesh=mesh, in_specs=in_specs, out_specs=out_specs, check_vma=False)
```
